256 devices in a mesh: tm: 32 (over z, y), state: 8 (over x, core).
Axes of the slice: x: 4, y: 4, z: 8, core: 2. Of those that a mesh axis runs over, the one named last changes fastest.
Arguments:
- observations: bfloat16 [512, 256, 384], P('tm', 'state'), may hold values from -6 to 6
- mask: int32 [512], P('tm'), may hold values 0 or 1
- transition: float32 [512, 512], P(None, 'state'), may hold values from -1 to 1
- updated_transition: float32 [512, 512], P(None, 'state'), may hold values from -1 to 1
- smoother_gain: float32 [512, 512], P(None, 'state'), may hold values from -1 to 1
- obs_gain: float32 [512, 384], replicated, may hold values from -0.02734375 to 0.02734375
- initial_mean: float32 [256, 512], P('state'), may hold values from -6 to 6
Outputs:
- filtered: float32 [512, 256, 512], P('tm', 'state')
- smoothed: float32 [512, 256, 512], P('tm', 'state')
The draws below stay inside these ranges and needn't reach their ends.
All inputs are finite; a program needn't handle non-finite values. No bound on the sum of `mask` on one device may be relied on, other than what follows from the above.
Results may differ from the reference program's by a relative error of at most 0.0003.
Values sent between devices are 32-bit elements; how exact they have to be, the bound alone decides.
No kernel may reach another device: no remote copies, remote signals or barrier semaphores. Data moves between devices by JAX's collectives and lax.ppermute only.
A program may use at most 256 MiB of HBM per device.

```python
import jax
import jax.numpy as jnp
from jax import lax

S = 512
C = 384
TIME = 512
TRIALS = 256


def dense_matrix(key, factor, share):
    part_one, part_two, part_three, part_four = jax.random.split(key, 4)
    slow = jax.random.uniform(part_one, (S,)) < share
    slow_rate = jax.random.uniform(part_two, (S,), minval=0.3, maxval=1.0) / TIME
    fast_rate = jax.random.uniform(part_three, (S,), minval=1.0 / 50.0, maxval=1.0 / 30.0)
    diagonal = jnp.exp(-factor * jnp.where(slow, slow_rate, fast_rate))
    outside = 1.0 - jnp.eye(S, dtype=jnp.float32)
    coupling = jax.random.normal(part_four, (S, S)) * outside
    row_total = jnp.sum(jnp.abs(coupling), axis=1) + 1e-06
    scale = 0.9 * (1.0 - diagonal) / row_total
    return coupling * scale[:, None] + jnp.eye(S, dtype=jnp.float32) * diagonal[:, None]


def draw_transition(key, part):
    key = jax.random.fold_in(key, 1)
    return dense_matrix(key, 1.0, 0.5)


def draw_updated_transition(key, part):
    key = jax.random.fold_in(key, 2)
    return dense_matrix(key, 2.0, 0.5)


def draw_smoother_gain(key, part):
    key = jax.random.fold_in(key, 3)
    return dense_matrix(key, 1.5, 0.5)


def place_ends(drawn, stream_key, least, largest):
    shape = drawn.shape
    place = [jax.random.randint(jax.random.fold_in(stream_key, axis), (), 0, shape[axis]) for axis in range(len(shape))]
    drawn = drawn.at[tuple(place)].set(least)
    longest = shape.index(max(shape))
    place[longest] = (place[longest] + 1) % shape[longest]
    return drawn.at[tuple(place)].set(largest)


def level_of(own_key, extent, pieces, low, high):
    level, own = 1.0, jax.random.fold_in(own_key, 6)
    for dim, parts in pieces:
        steps = jnp.exp(jax.random.uniform(jax.random.fold_in(own, dim), (parts,), jnp.float32, low / len(pieces), high / len(pieces)))
        level = level * jnp.repeat(steps, extent[dim] // parts).reshape([-1 if axis == dim else 1 for axis in range(len(extent))])
    return level


def scatter_about(rng, dims, spread, most, cuts=(), held_as=jnp.bfloat16):
    result = spread * jax.random.normal(rng, dims, jnp.float32)
    if cuts:
        result = result * level_of(rng, dims, cuts, -0.22, 0.18)
    return jnp.clip(result, -most, most).astype(held_as)


def setup_inputs(seed: int = 0) -> dict:
    key_list = jax.random.split(jax.random.key(seed), 8)
    return {
        "observations": scatter_about(key_list[0], (TIME, TRIALS, C), 1.0, 6.0, ((0, 32), (1, 8))),
        "mask": place_ends((jax.random.randint(key_list[1], (TIME,), 0, 4) < 3).astype(jnp.int32), jax.random.fold_in(key_list[1], 1), 0, 1),
        "transition": draw_transition(jax.random.fold_in(key_list[7], 71), 0),
        "updated_transition": draw_updated_transition(jax.random.fold_in(key_list[7], 71), 0),
        "smoother_gain": draw_smoother_gain(jax.random.fold_in(key_list[7], 71), 0),
        "obs_gain": scatter_about(key_list[5], (S, C), (C * TIME // 4) ** -0.5, 0.02734375, (), jnp.float32),
        "initial_mean": scatter_about(key_list[6], (TRIALS, S), 1.0, 6.0, ((0, 8),), jnp.float32),
    }


def times_transpose(left, right):
    return lax.dot_general(left, right, (((1,), (1,)), ((), ())), precision=lax.Precision.HIGHEST, preferred_element_type=jnp.float32)


def reference(observations, mask, transition, updated_transition, smoother_gain, obs_gain, initial_mean):
    def forward_step(mean, inputs):
        frame, flag = inputs
        chosen = jnp.where(flag > 0, updated_transition, transition)
        drive = times_transpose(frame.astype(jnp.float32), obs_gain) * flag.astype(jnp.float32)
        mean = times_transpose(mean, chosen) + drive
        return mean, mean

    filtered = lax.scan(forward_step, initial_mean, (observations, mask))[1]
    virtual = times_transpose(filtered[-1], transition)

    def backward_step(later, current):
        gap = current - times_transpose(times_transpose(current, transition), smoother_gain)
        value = times_transpose(later, smoother_gain) + gap
        return value, value

    smoothed = lax.scan(backward_step, virtual, filtered, reverse=True)[1]
    return filtered, smoothed
```

```python
import functools

import jax
import jax.numpy as jnp
from jax import lax
from jax.experimental import pallas as pl
from jax.experimental.pallas import tpu as pltpu
from jax.sharding import PartitionSpec as P

F32 = jnp.float32
BF16 = jnp.bfloat16
VMEM = pl.BlockSpec(memory_space=pltpu.VMEM)
SMEM = pl.BlockSpec(memory_space=pltpu.SMEM)
LIMIT = 50 * 1024 * 1024


def split(a):
    high = a.astype(BF16)
    return high, (a - high.astype(F32)).astype(BF16)


def dot(left, right):
    return jnp.dot(left, right, preferred_element_type=F32)


def dot3(a, high, low):
    rows = a.shape[0]
    a_high, a_low = split(a)
    both = dot(jnp.concatenate([a_high, a_low], 0), high)
    return both[:rows] + both[rows:] + dot(a_high, low)


def call(kernel, outs, specs, args, name, flops, scratch=()):
    return pl.pallas_call(
        kernel,
        out_shape=outs,
        in_specs=specs,
        out_specs=jax.tree.map(lambda _: VMEM, outs),
        scratch_shapes=list(scratch),
        compiler_params=pltpu.CompilerParams(vmem_limit_bytes=LIMIT),
        cost_estimate=pl.CostEstimate(flops=flops, bytes_accessed=4 << 20, transcendentals=0),
        name=name,
    )(*args)


def shape(*dims, dtype=F32):
    return jax.ShapeDtypeStruct(dims, dtype)


def drive_kernel(mask_ref, frames_ref, gain_ref, out_ref):
    high, low = split(gain_ref[...])
    frames = frames_ref[...]
    turned = (((1,), (1,)), ((), ()))
    drive = lax.dot_general(frames, high, turned, preferred_element_type=F32)
    drive = drive + lax.dot_general(frames, low, turned, preferred_element_type=F32)
    steps, trials, _ = out_ref.shape
    for t in range(steps):
        out_ref[t] = drive[t * trials : (t + 1) * trials] * mask_ref[t].astype(F32)


def local_kernel(place_ref, mask_ref, *refs):
    pieces, (drive_ref, start_ref, last_ref, high_ref, low_ref) = refs[:8], refs[8:]
    panel, width = pieces[0].shape[1:]
    for i, piece in enumerate(pieces):
        row = pl.multiple_of(place_ref[i] * panel, panel)
        across = lax.broadcasted_iota(jnp.int32, (panel, width), 1)
        down = lax.broadcasted_iota(jnp.int32, (panel, width), 0) + row
        eye = jnp.where(across == down, 1.0, 0.0).astype(F32)
        for m in range(2):
            high, low = split(piece[m] - eye)
            high_ref[m, pl.ds(row, panel), :] = high
            low_ref[m, pl.ds(row, panel), :] = low

    def step(t, mean):
        m = mask_ref[t]
        return mean + dot3(mean, high_ref[m], low_ref[m]) + drive_ref[t]

    last_ref[...] = lax.fori_loop(0, drive_ref.shape[0], step, start_ref[...])


def table_kernel(core_ref, pattern_ref, high_ref, low_ref, l1_ref, l2_ref, l3_ref, l4_ref, near_ref, v4_ref, v8_ref,
                 ph_ref, pl_ref, th_ref, tl_ref):
    width = high_ref.shape[1]

    def compose(eh, el, lh, ll):
        product = dot(eh, lh) + dot(el, lh) + dot(eh, ll)
        whole = eh.astype(F32) + el.astype(F32) + lh.astype(F32) + ll.astype(F32)
        return split(product + whole)

    def pair(i, _):
        first, second = lax.rem(i, 2), lax.div(i, 2)
        high, low = compose(high_ref[first], low_ref[first], high_ref[second], low_ref[second])
        ph_ref[i], pl_ref[i] = high, low
        return 0

    lax.fori_loop(0, 4, pair, 0)

    def quad(i, _):
        first, second = lax.rem(i, 4), lax.div(i, 4)
        high, low = compose(ph_ref[first], pl_ref[first], ph_ref[second], pl_ref[second])
        th_ref[i], tl_ref[i] = high, low
        return 0

    lax.fori_loop(0, 16, quad, 0)
    th_ref[16] = jnp.zeros((width, width), BF16)
    tl_ref[16] = jnp.zeros((width, width), BF16)

    quads = pattern_ref.shape[0]
    near = l4_ref[...]
    for block, later in enumerate((l3_ref, l2_ref, l1_ref)):

        def forward(i, mean, block=block):
            q = pattern_ref[quads - 12 + 4 * block + i]
            return mean + dot3(mean, th_ref[q], tl_ref[q])

        near = lax.fori_loop(0, 4, forward, near) + later[...]
    near_ref[...] = near

    half = v8_ref.shape[1]
    across = lax.broadcasted_iota(jnp.int32, (width, half), 1) + core_ref[0] * half
    down = lax.broadcasted_iota(jnp.int32, (width, half), 0)
    v8_ref[...] = jnp.where(across == down, 1.0, 0.0).astype(F32)

    def extend(i, _):
        q = pattern_ref[quads - 1 - i]
        high, low = split(v8_ref[...])
        v8_ref[...] += dot(th_ref[q], high) + dot(tl_ref[q], high) + dot(th_ref[q], low)
        return 0

    lax.fori_loop(0, 16, extend, 0)
    v4_ref[...] = v8_ref[...]
    lax.fori_loop(16, 32, extend, 0)


def powers_kernel(gain_ref, fh_ref, fl_ref, gh_ref, gl_ref, g4h_ref, g4l_ref, kh_ref, kl_ref, far_ref, now_ref):
    width = gain_ref.shape[0]
    across = lax.broadcasted_iota(jnp.int32, (width, width), 1)
    down = lax.broadcasted_iota(jnp.int32, (width, width), 0)
    now_ref[...] = gain_ref[...] - jnp.where(across == down, 1.0, 0.0).astype(F32)
    high, low = split(now_ref[...])
    gh_ref[...], gl_ref[...] = high, low
    product = dot(fh_ref[0], high) + dot(fl_ref[0], high) + dot(fh_ref[0], low)
    both = fh_ref[0].astype(F32) + fl_ref[0].astype(F32) + now_ref[...]
    kh_ref[...], kl_ref[...] = split(product + both)

    def square(i, _):
        high, low = split(now_ref[...])
        now_ref[...] = 2.0 * now_ref[...] + dot(high, high) + dot(low, high) + dot(high, low)

        @pl.when(i == 1)
        def _():
            g4h_ref[...], g4l_ref[...] = split(now_ref[...])

        @pl.when(i >= 3)
        def _():
            far_ref[i - 3] = now_ref[...]

        return 0

    lax.fori_loop(0, 8, square, 0)


def forward_kernel(mask_ref, final_ref, start_ref, drive_ref, bh_ref, bl_ref, gh_ref, gl_ref, g4h_ref, g4l_ref, kh_ref,
                   kl_ref, filtered_ref, gap_ref, part_ref, back_ref, virtual_ref):
    steps, trials, width = drive_ref.shape
    groups, inner = gap_ref.shape[:2]

    def step(t, mean):
        m = mask_ref[t]
        mean = mean + dot3(mean, bh_ref[m], bl_ref[m]) + drive_ref[t]
        filtered_ref[t] = mean
        return mean

    last = lax.fori_loop(0, steps, step, start_ref[...])
    virtual = last + dot3(last, bh_ref[0], bl_ref[0])
    virtual_ref[...] = virtual
    for g in range(groups):
        flat = filtered_ref[g * inner : (g + 1) * inner].reshape(inner * trials, width)
        gap_ref[g] = -dot3(flat, kh_ref[...], kl_ref[...]).reshape(inner, trials, width)
    value = gap_ref[:, inner - 1].reshape(groups * trials, width)
    for j in range(inner - 2, -1, -1):
        value = value + dot3(value, gh_ref[...], gl_ref[...]) + gap_ref[:, j].reshape(groups * trials, width)
    part = value.reshape(groups, trials, width)
    part_ref[...] = part
    carry = jnp.where(final_ref[0] > 0, virtual, jnp.zeros_like(virtual))
    for g in range(groups - 1, -1, -1):
        carry = carry + dot3(carry, g4h_ref[...], g4l_ref[...]) + part[g]
    back_ref[...] = carry


def backward_kernel(start_ref, gap_ref, part_ref, gh_ref, gl_ref, g4h_ref, g4l_ref, out_ref):
    groups, inner, trials, width = gap_ref.shape
    carry = start_ref[...]
    starts = [carry]
    for g in range(groups - 1, 0, -1):
        carry = carry + dot3(carry, g4h_ref[...], g4l_ref[...]) + part_ref[g]
        starts.insert(0, carry)
    value = jnp.concatenate(starts, 0)
    for j in range(inner - 1, -1, -1):
        value = value + dot3(value, gh_ref[...], gl_ref[...]) + gap_ref[:, j].reshape(groups * trials, width)
        out_ref[:, j] = value.reshape(groups, trials, width)


def high_dot(left, right):
    return jnp.dot(left, right, precision=lax.Precision.HIGH, preferred_element_type=F32)


def local(observations, mask, transition, updated_transition, smoother_gain, obs_gain, initial_mean):
    steps, trials, channels = observations.shape
    width, panel = transition.shape
    count = lax.axis_size("tm")
    chips = lax.axis_size("state") // 2
    block = lax.axis_index("tm")
    place = lax.axis_index("state")
    chip, core = place // 2, place % 2

    def along_x(a, k):
        return lax.ppermute(
            a, "state", [(2 * i + c, 2 * ((i + k) % chips) + c) for i in range(chips) for c in range(2)]
        )

    def swap(a):
        return lax.ppermute(a, "state", [(2 * i + c, 2 * i + 1 - c) for i in range(chips) for c in range(2)])

    def later(a, k):
        moved = lax.ppermute(a, "tm", [(i, (i + k) % count) for i in range(count)])
        return jnp.where(block >= k, moved, jnp.zeros_like(moved))

    own = jnp.stack([transition.T, updated_transition.T])
    mine = [own] + [along_x(own, k) for k in (1, 2, 3)]
    theirs = [swap(a) for a in mine]
    sources = jnp.stack([(chip - k) % chips for k in range(4)])
    places = jnp.concatenate([2 * sources + core, 2 * sources + 1 - core]).astype(jnp.int32)
    gain = lax.all_gather(smoother_gain.T, "state", axis=0, tiled=True)

    quads = steps // 4
    code = jnp.sum(mask.reshape(quads, 4) * jnp.array([1, 2, 4, 8], jnp.int32), axis=1)
    codes = lax.all_to_all(jnp.tile(code[None], (count, 1)), "tm", 0, 0, tiled=True).reshape(count * quads)
    padded = jnp.concatenate([jnp.full((8 * quads,), 16, jnp.int32), codes])
    patterns = lax.dynamic_slice_in_dim(padded, quads * block, 8 * quads, 0)

    drive = call(
        drive_kernel,
        shape(steps, trials, width),
        [SMEM, VMEM, VMEM],
        (mask, observations.reshape(steps * trials, channels), obs_gain),
        "drive",
        4 * steps * trials * channels * width,
    )

    square = width * width
    start = jnp.where(block == 0, initial_mean, jnp.zeros_like(initial_mean))
    last, bh, bl = call(
        local_kernel,
        (shape(trials, width), shape(2, width, width, dtype=BF16), shape(2, width, width, dtype=BF16)),
        [SMEM, SMEM] + [VMEM] * 10,
        (places, mask, *mine, *theirs, drive, start),
        "local",
        60 * trials * steps * square // 4,
    )
    before = [later(last, k) for k in (1, 2, 3, 4)]
    half = width // 2
    near, v4, v8 = call(
        table_kernel,
        (shape(trials, width), shape(width, half), shape(width, half)),
        [SMEM, SMEM] + [VMEM] * 6,
        (core.reshape(1).astype(jnp.int32), patterns, bh, bl, *before),
        "table",
        6 * 20 * square * width,
        (
            pltpu.VMEM((4, width, width), BF16),
            pltpu.VMEM((4, width, width), BF16),
            pltpu.VMEM((17, width, width), BF16),
            pltpu.VMEM((17, width, width), BF16),
        ),
    )
    v4_other, v8_other = swap(v4), swap(v8)

    def apply(mean, mine, theirs):
        here, there = high_dot(mean, mine), high_dot(mean, theirs)
        return jnp.where(
            core == 0, jnp.concatenate([here, there], 1), jnp.concatenate([there, here], 1)
        )

    mean = near + apply(later(near, 4), v4, v4_other)
    reach = mean
    for _ in range(3):
        mean = reach + apply(later(mean, 8), v8, v8_other)
    mean = jnp.where(block == 0, initial_mean, mean)

    bf = functools.partial(shape, width, width, dtype=BF16)
    gh, gl, g4h, g4l, kh, kl, far = call(
        powers_kernel,
        (bf(), bf(), bf(), bf(), bf(), bf(), shape(5, width, width)),
        [VMEM] * 3,
        (gain, bh, bl),
        "powers",
        6 * 9 * square * width,
        (pltpu.VMEM((width, width), F32),),
    )

    final = block == count - 1
    filtered, gap, part, back, virtual = call(
        forward_kernel,
        (
            shape(steps, trials, width),
            shape(4, steps // 4, trials, width),
            shape(4, trials, width),
            shape(trials, width),
            shape(trials, width),
        ),
        [SMEM, SMEM] + [VMEM] * 10,
        (mask, final.reshape(1).astype(jnp.int32), mean, drive, bh, bl, gh, gl, g4h, g4l, kh, kl),
        "forward",
        60 * trials * steps * square // 4,
    )

    scan = lax.all_to_all(back, "tm", 0, 0, tiled=True)
    for k in range(5):
        ahead = jnp.concatenate([scan[2**k :], jnp.zeros((2**k, width), F32)], 0)
        scan = scan + ahead + high_dot(ahead, far[k])
    ahead = jnp.concatenate([scan[1:], jnp.zeros((1, width), F32)], 0)
    back_in = lax.all_to_all(ahead, "tm", 0, 0, tiled=True)
    smoothed = call(
        backward_kernel,
        shape(4, steps // 4, trials, width),
        [VMEM] * 7,
        (jnp.where(final, virtual, back_in), gap, part, gh, gl, g4h, g4l),
        "backward",
        60 * trials * steps * square // 4,
    )
    return filtered, smoothed.reshape(steps, trials, width)


def solution(mesh):
    placed = (
        P("tm", "state", None),
        P("tm"),
        P(None, "state"),
        P(None, "state"),
        P(None, "state"),
        P(),
        P("state", None),
    )
    return jax.shard_map(
        local,
        mesh=mesh,
        in_specs=placed,
        out_specs=(P("tm", "state", None), P("tm", "state", None)),
        check_vma=False,
    )
```

```python
import functools

import jax
import jax.numpy as jnp
from jax import lax
from jax.experimental import pallas as pl
from jax.experimental.pallas import tpu as pltpu
from jax.sharding import PartitionSpec as P

F32 = jnp.float32
BF16 = jnp.bfloat16
VMEM = pl.BlockSpec(memory_space=pltpu.VMEM)
SMEM = pl.BlockSpec(memory_space=pltpu.SMEM)
LIMIT = 16 * 1024 * 1024


def split(a):
    high = a.astype(BF16)
    return high, (a - high.astype(F32)).astype(BF16)


def dot(left, right):
    return jnp.dot(left, right, preferred_element_type=F32)


def dot3(a, high, low):
    rows = a.shape[0]
    a_high, a_low = split(a)
    both = dot(jnp.concatenate([a_high, a_low], 0), high)
    return both[:rows] + both[rows:] + dot(a_high, low)


def call(kernel, outs, specs, args, name, micros, scratch=()):
    return pl.pallas_call(
        kernel,
        out_shape=outs,
        in_specs=specs,
        out_specs=jax.tree.map(lambda _: VMEM, outs),
        scratch_shapes=list(scratch),
        compiler_params=pltpu.CompilerParams(vmem_limit_bytes=LIMIT),
        cost_estimate=pl.CostEstimate(flops=int(micros * 1.15e9), bytes_accessed=1 << 20, transcendentals=0),
        name=name,
    )(*args)


def shape(*dims, dtype=F32):
    return jax.ShapeDtypeStruct(dims, dtype)


def drive_kernel(mask_ref, frames_ref, gain_ref, out_ref):
    high, low = split(gain_ref[...])
    frames = frames_ref[...]
    turned = (((1,), (1,)), ((), ()))
    drive = lax.dot_general(frames, high, turned, preferred_element_type=F32)
    drive = drive + lax.dot_general(frames, low, turned, preferred_element_type=F32)
    steps, trials, _ = out_ref.shape
    for t in range(steps):
        out_ref[t] = drive[t * trials : (t + 1) * trials] * mask_ref[t].astype(F32)


def gathered(place_ref, pieces, write):
    panel, width = pieces[0].shape[-2:]
    for i, piece in enumerate(pieces):
        row = pl.multiple_of(place_ref[i] * panel, panel)
        across = lax.broadcasted_iota(jnp.int32, (panel, width), 1)
        down = lax.broadcasted_iota(jnp.int32, (panel, width), 0) + row
        write(pl.ds(row, panel), piece, jnp.where(across == down, 1.0, 0.0).astype(F32))


def compose(eh, el, lh, ll):
    product = dot(eh, lh) + dot(el, lh) + dot(eh, ll)
    whole = eh.astype(F32) + el.astype(F32) + lh.astype(F32) + ll.astype(F32)
    return split(product + whole)


def chosen_step(rows, flags, high_ref, low_ref):
    parts = [dot3(rows, high_ref[m], low_ref[m]) for m in range(2)]
    size = rows.shape[0] // len(flags)
    return [
        jnp.where(flag > 0, parts[1][i * size : (i + 1) * size], parts[0][i * size : (i + 1) * size])
        for i, flag in enumerate(flags)
    ]


def local_kernel(place_ref, mask_ref, *refs):
    pieces, (drive_ref, start_ref, last_ref, input_ref, high_ref, low_ref, pair_ref) = refs[:8], refs[8:]
    pairs, trials, width = input_ref.shape

    def write(rows, piece, eye):
        for m in range(2):
            high, low = split(piece[m] - eye)
            high_ref[m, rows, :] = high
            low_ref[m, rows, :] = low

    gathered(place_ref, pieces, write)

    def pair(i, _):
        first, second = lax.rem(i, 2), lax.div(i, 2)
        pair_ref[i, 0], pair_ref[i, 1] = compose(high_ref[first], low_ref[first], high_ref[second], low_ref[second])
        return 0

    lax.fori_loop(0, 4, pair, 0)
    for start in range(0, pairs, 4):
        some = range(start, start + 4)
        rows = jnp.concatenate([drive_ref[2 * i] for i in some], 0)
        moved = chosen_step(rows, [mask_ref[2 * i + 1] for i in some], high_ref, low_ref)
        for i, part in zip(some, moved):
            input_ref[i] = drive_ref[2 * i] + part + drive_ref[2 * i + 1]

    def step(i, mean):
        p = mask_ref[2 * i] + 2 * mask_ref[2 * i + 1]
        return mean + dot3(mean, pair_ref[p, 0], pair_ref[p, 1]) + input_ref[i]

    last_ref[...] = lax.fori_loop(0, pairs, step, start_ref[...])


def window_kernel(begin, count, core_ref, pattern_ref, pair_ref, *refs):
    out_ref = refs[-1]
    width, half = out_ref.shape
    if begin == 0:
        across = lax.broadcasted_iota(jnp.int32, (width, half), 1) + core_ref[0] * half
        down = lax.broadcasted_iota(jnp.int32, (width, half), 0)
        out_ref[...] = jnp.where(across == down, 1.0, 0.0).astype(F32)
    else:
        out_ref[...] = refs[0][...]
    end = pattern_ref.shape[0] - 1 - begin

    def step(i, _):
        p = pattern_ref[end - i]

        @pl.when(p < 4)
        def _():
            high, low = split(out_ref[...])
            out_ref[...] += dot(pair_ref[p, 0], high) + dot(pair_ref[p, 1], high) + dot(pair_ref[p, 0], low)

        return 0

    lax.fori_loop(0, count, step, 0)


def square(ref):
    high, low = split(ref[...])
    ref[...] = 2.0 * ref[...] + dot(high, high) + dot(low, high) + dot(high, low)


def powers_kernel(place_ref, *refs):
    pieces = refs[:8]
    fh_ref, fl_ref, gh_ref, gl_ref, g4h_ref, g4l_ref, kh_ref, kl_ref, now_ref = refs[8:]

    def write(rows, piece, eye):
        now_ref[rows, :] = piece[...] - eye

    gathered(place_ref, pieces, write)
    high, low = split(now_ref[...])
    gh_ref[...], gl_ref[...] = high, low
    product = dot(fh_ref[0], high) + dot(fl_ref[0], high) + dot(fh_ref[0], low)
    both = fh_ref[0].astype(F32) + fl_ref[0].astype(F32) + now_ref[...]
    kh_ref[...], kl_ref[...] = split(product + both)
    square(now_ref)
    square(now_ref)
    g4h_ref[...], g4l_ref[...] = split(now_ref[...])


def middle_kernel(now_ref, p1_ref, p2_ref):
    p1_ref[...] = now_ref[...]
    square(p1_ref)
    square(p1_ref)
    p2_ref[...] = p1_ref[...]
    square(p2_ref)


def far_kernel(p2_ref, p4_ref, p8_ref, p16_ref):
    p4_ref[...] = p2_ref[...]
    square(p4_ref)
    p8_ref[...] = p4_ref[...]
    square(p8_ref)
    p16_ref[...] = p8_ref[...]
    square(p16_ref)


def forward_kernel(mask_ref, final_ref, start_ref, drive_ref, input_ref, pair_ref, bh_ref, bl_ref, gh_ref, gl_ref,
                   g4h_ref, g4l_ref, kh_ref, kl_ref, filtered_ref, gap_ref, part_ref, back_ref, virtual_ref):
    steps, trials, width = drive_ref.shape
    groups, inner = gap_ref.shape[:2]

    def step(i, mean):
        p = mask_ref[2 * i] + 2 * mask_ref[2 * i + 1]
        mean = mean + dot3(mean, pair_ref[p, 0], pair_ref[p, 1]) + input_ref[i]
        filtered_ref[2 * i + 1] = mean
        return mean

    last = lax.fori_loop(0, steps // 2, step, start_ref[...])
    for start in range(0, steps, 8):
        some = range(start, start + 8, 2)
        rows = [start_ref[...] if t == 0 else filtered_ref[t - 1] for t in some]
        moved = chosen_step(jnp.concatenate(rows, 0), [mask_ref[t] for t in some], bh_ref, bl_ref)
        for t, row, part in zip(some, rows, moved):
            filtered_ref[t] = row + part + drive_ref[t]
    virtual = last + dot3(last, bh_ref[0], bl_ref[0])
    virtual_ref[...] = virtual
    for g in range(groups):
        flat = filtered_ref[g * inner : (g + 1) * inner].reshape(inner * trials, width)
        gap_ref[g] = -dot3(flat, kh_ref[...], kl_ref[...]).reshape(inner, trials, width)
    value = gap_ref[:, inner - 1].reshape(groups * trials, width)
    for j in range(inner - 2, -1, -1):
        value = value + dot3(value, gh_ref[...], gl_ref[...]) + gap_ref[:, j].reshape(groups * trials, width)
    part = value.reshape(groups, trials, width)
    part_ref[...] = part
    carry = jnp.where(final_ref[0] > 0, virtual, jnp.zeros_like(virtual))
    for g in range(groups - 1, -1, -1):
        carry = carry + dot3(carry, g4h_ref[...], g4l_ref[...]) + part[g]
    back_ref[...] = carry


def backward_kernel(start_ref, gap_ref, part_ref, gh_ref, gl_ref, g4h_ref, g4l_ref, out_ref):
    groups, inner, trials, width = gap_ref.shape
    carry = start_ref[...]
    starts = [carry]
    for g in range(groups - 1, 0, -1):
        carry = carry + dot3(carry, g4h_ref[...], g4l_ref[...]) + part_ref[g]
        starts.insert(0, carry)
    value = jnp.concatenate(starts, 0)
    for j in range(inner - 1, -1, -1):
        value = value + dot3(value, gh_ref[...], gl_ref[...]) + gap_ref[:, j].reshape(groups * trials, width)
        out_ref[:, j] = value.reshape(groups, trials, width)


def high_dot(left, right):
    return jnp.dot(left, right, precision=lax.Precision.HIGH, preferred_element_type=F32)


def local(observations, mask, transition, updated_transition, smoother_gain, obs_gain, initial_mean):
    steps, trials, channels = observations.shape
    width, panel = transition.shape
    count = lax.axis_size("tm")
    chips = lax.axis_size("state") // 2
    block = lax.axis_index("tm")
    place = lax.axis_index("state")
    chip, core = place // 2, place % 2

    def along_x(a, k):
        return lax.ppermute(
            a, "state", [(2 * i + c, 2 * ((i + k) % chips) + c) for i in range(chips) for c in range(2)]
        )

    def swap(a):
        return lax.ppermute(a, "state", [(2 * i + c, 2 * i + 1 - c) for i in range(chips) for c in range(2)])

    def shifted(a, k):
        return lax.ppermute(a, "tm", [(i, (i + k) % count) for i in range(count)])

    codes = mask.reshape(steps // 2, 2) @ jnp.array([1, 2], jnp.int32)

    def earlier(a, k):
        return jnp.where(block >= k, shifted(a, k), 4)

    pattern = jnp.concatenate([earlier(codes, 2), earlier(codes, 1)])
    pattern = jnp.concatenate([earlier(pattern, 2), pattern])
    pattern = jnp.concatenate([earlier(pattern, 4), pattern])

    def pieces(own):
        mine = [own] + [along_x(own, k) for k in (1, 2, 3)]
        return mine, [swap(a) for a in mine]

    mine, theirs = pieces(jnp.stack([transition.T, updated_transition.T]))
    sources = jnp.stack([(chip - k) % chips for k in range(4)])
    places = jnp.concatenate([2 * sources + core, 2 * sources + 1 - core]).astype(jnp.int32)

    drive = call(
        drive_kernel,
        shape(steps, trials, width),
        [SMEM, VMEM, VMEM],
        (mask, observations.reshape(steps * trials, channels), obs_gain),
        "drive",
        2,
    )

    start = jnp.where(block == 0, initial_mean, jnp.zeros_like(initial_mean))
    bf = functools.partial(shape, width, width, dtype=BF16)
    two = shape(2, width, width, dtype=BF16)
    pattern, places = lax.optimization_barrier((pattern, places))
    last, inputs, bh, bl, pair = call(
        local_kernel,
        (shape(trials, width), shape(steps // 2, trials, width), two, two, shape(4, 2, width, width, dtype=BF16)),
        [SMEM, SMEM] + [VMEM] * 10,
        (places, mask, *mine, *theirs, drive, start),
        "local",
        9,
    )

    half = width // 2
    cores = core.reshape(1).astype(jnp.int32)

    def window(begin, count, *first):
        return call(
            functools.partial(window_kernel, begin, count),
            shape(width, half),
            [SMEM, SMEM, VMEM] + [VMEM] * len(first),
            (cores, pattern, pair, *first),
            f"window{begin + count}",
            0.6 * count,
        )

    def apply(mean, k, mine, theirs):
        mean = jnp.where(block >= k, mean, 0.0)
        here, there = high_dot(mean, mine), high_dot(mean, theirs)
        return jnp.where(
            core == 0, jnp.concatenate([here, there], 1), jnp.concatenate([there, here], 1)
        )

    one, two_back = shifted(last, 1), shifted(last, 2)
    v1 = window(0, 8)
    v1_other = swap(v1)
    v2 = window(8, 8, v1)
    v1, v1_other, v2 = lax.optimization_barrier((v1, v1_other, v2))
    reach = jnp.where(block >= 1, one, 0.0) + apply(two_back, 2, v1, v1_other)

    reach, v2 = lax.optimization_barrier((reach, v2))
    moved = shifted(reach, 2)
    v2_other = swap(v2)
    v4 = window(16, 8, v2)
    v2, v2_other, v4 = lax.optimization_barrier((v2, v2_other, v4))
    reach = reach + apply(moved, 2, v2, v2_other)

    reach, v4 = lax.optimization_barrier((reach, v4))
    moved = shifted(reach, 4)
    v4 = window(24, 8, v4)
    v4_other = swap(v4)
    v8 = window(32, 8, v4)
    v4, v4_other, v8 = lax.optimization_barrier((v4, v4_other, v8))
    reach = reach + apply(moved, 4, v4, v4_other)

    reach, v8 = lax.optimization_barrier((reach, v8))
    moved = shifted(reach, 8)
    v8 = window(40, 12, v8)
    ready, v2 = lax.optimization_barrier((smoother_gain.T, v2))
    gain_mine, gain_theirs = pieces(ready)
    moved, v8, *gain = lax.optimization_barrier((moved, v8, *gain_mine, *gain_theirs))
    v8 = window(52, 12, v8)
    v8_other = swap(v8)
    mean = reach + apply(moved, 8, v8, v8_other)
    gain[0], mean = lax.optimization_barrier((gain[0], mean))
    for _ in range(2):
        mean = reach + apply(shifted(mean, 8), 8, v8, v8_other)
    mean = jnp.where(block == 0, initial_mean, mean)

    gh, gl, g4h, g4l, kh, kl, g4 = call(
        powers_kernel,
        (bf(), bf(), bf(), bf(), bf(), bf(), shape(width, width)),
        [SMEM] + [VMEM] * 10,
        (places, *gain, bh, bl),
        "powers",
        4,
    )
    p1, p2 = call(middle_kernel, (shape(width, width),) * 2, [VMEM], (g4,), "middle", 4)
    p4, p8, p16 = call(far_kernel, (shape(width, width),) * 3, [VMEM], (p2,), "far", 4)
    far = (p1, p2, p4, p8, p16)

    final = block == count - 1
    filtered, gap, part, back, virtual = call(
        forward_kernel,
        (
            shape(steps, trials, width),
            shape(4, steps // 4, trials, width),
            shape(4, trials, width),
            shape(trials, width),
            shape(trials, width),
        ),
        [SMEM, SMEM] + [VMEM] * 12,
        (mask, final.reshape(1).astype(jnp.int32), mean, drive, inputs, pair, bh, bl, gh, gl, g4h, g4l, kh, kl),
        "forward",
        10,
    )

    scan = lax.all_to_all(back, "tm", 0, 0, tiled=True)
    for k in range(5):
        ahead = jnp.concatenate([scan[2**k :], jnp.zeros((2**k, width), F32)], 0)
        scan = scan + ahead + high_dot(ahead, far[k])
    ahead = jnp.concatenate([scan[1:], jnp.zeros((1, width), F32)], 0)
    back_in = lax.all_to_all(ahead, "tm", 0, 0, tiled=True)
    smoothed = call(
        backward_kernel,
        shape(4, steps // 4, trials, width),
        [VMEM] * 7,
        (jnp.where(final, virtual, back_in), gap, part, gh, gl, g4h, g4l),
        "backward",
        3,
    )
    return filtered, smoothed.reshape(steps, trials, width)


def solution(mesh):
    placed = (
        P("tm", "state", None),
        P("tm"),
        P(None, "state"),
        P(None, "state"),
        P(None, "state"),
        P(),
        P("state", None),
    )
    return jax.shard_map(
        local,
        mesh=mesh,
        in_specs=placed,
        out_specs=(P("tm", "state", None), P("tm", "state", None)),
        check_vma=False,
    )
```

```python
import functools

import jax
import jax.numpy as jnp
from jax import lax
from jax.experimental import pallas as pl
from jax.experimental.pallas import tpu as pltpu
from jax.sharding import PartitionSpec as P

F32 = jnp.float32
BF16 = jnp.bfloat16
VMEM = pl.BlockSpec(memory_space=pltpu.VMEM)
SMEM = pl.BlockSpec(memory_space=pltpu.SMEM)
LIMIT = 12 * 1024 * 1024


def split(a):
    high = a.astype(BF16)
    return high, (a - high.astype(F32)).astype(BF16)


def dot(left, right):
    return jnp.dot(left, right, preferred_element_type=F32)


def dot3(a, high, low):
    rows = a.shape[0]
    a_high, a_low = split(a)
    both = dot(jnp.concatenate([a_high, a_low], 0), high)
    return both[:rows] + both[rows:] + dot(a_high, low)


def call(kernel, outs, specs, args, name, micros, scratch=()):
    return pl.pallas_call(
        kernel,
        out_shape=outs,
        in_specs=specs,
        out_specs=jax.tree.map(lambda _: VMEM, outs),
        scratch_shapes=list(scratch),
        compiler_params=pltpu.CompilerParams(vmem_limit_bytes=LIMIT),
        cost_estimate=pl.CostEstimate(flops=int(micros * 5e7), bytes_accessed=1 << 20, transcendentals=0),
        name=name,
    )(*args)


def shape(*dims, dtype=F32):
    return jax.ShapeDtypeStruct(dims, dtype)


def drive_kernel(mask_ref, frames_ref, gain_ref, out_ref):
    high, low = split(gain_ref[...])
    frames = frames_ref[...]
    turned = (((1,), (1,)), ((), ()))
    drive = lax.dot_general(frames, high, turned, preferred_element_type=F32)
    drive = drive + lax.dot_general(frames, low, turned, preferred_element_type=F32)
    steps, trials, _ = out_ref.shape
    for t in range(steps):
        out_ref[t] = drive[t * trials : (t + 1) * trials] * mask_ref[t].astype(F32)


def gathered(place_ref, pieces, write):
    panel, width = pieces[0].shape[-2:]
    for i, piece in enumerate(pieces):
        row = pl.multiple_of(place_ref[i] * panel, panel)
        across = lax.broadcasted_iota(jnp.int32, (panel, width), 1)
        down = lax.broadcasted_iota(jnp.int32, (panel, width), 0) + row
        write(pl.ds(row, panel), piece, jnp.where(across == down, 1.0, 0.0).astype(F32))


def compose(eh, el, lh, ll):
    product = dot(eh, lh) + dot(el, lh) + dot(eh, ll)
    whole = eh.astype(F32) + el.astype(F32) + lh.astype(F32) + ll.astype(F32)
    return split(product + whole)


def chosen_step(rows, flags, high_ref, low_ref):
    parts = [dot3(rows, high_ref[m], low_ref[m]) for m in range(2)]
    size = rows.shape[0] // len(flags)
    return [
        jnp.where(flag > 0, parts[1][i * size : (i + 1) * size], parts[0][i * size : (i + 1) * size])
        for i, flag in enumerate(flags)
    ]


def local_kernel(place_ref, mask_ref, *refs):
    pieces, (drive_ref, start_ref, last_ref, input_ref, high_ref, low_ref, pair_ref) = refs[:8], refs[8:]
    pairs, trials, width = input_ref.shape

    def write(rows, piece, eye):
        for m in range(2):
            high, low = split(piece[m] - eye)
            high_ref[m, rows, :] = high
            low_ref[m, rows, :] = low

    gathered(place_ref, pieces, write)

    def pair(i, _):
        first, second = lax.rem(i, 2), lax.div(i, 2)
        pair_ref[i, 0], pair_ref[i, 1] = compose(high_ref[first], low_ref[first], high_ref[second], low_ref[second])
        return 0

    lax.fori_loop(0, 4, pair, 0)
    for start in range(0, pairs, 4):
        some = range(start, start + 4)
        rows = jnp.concatenate([drive_ref[2 * i] for i in some], 0)
        moved = chosen_step(rows, [mask_ref[2 * i + 1] for i in some], high_ref, low_ref)
        for i, part in zip(some, moved):
            input_ref[i] = drive_ref[2 * i] + part + drive_ref[2 * i + 1]

    def step(i, mean):
        p = mask_ref[2 * i] + 2 * mask_ref[2 * i + 1]
        return mean + dot3(mean, pair_ref[p, 0], pair_ref[p, 1]) + input_ref[i]

    last_ref[...] = lax.fori_loop(0, pairs, step, start_ref[...])


def window_kernel(begin, count, core_ref, pattern_ref, pair_ref, *refs):
    out_ref = refs[-1]
    width, half = out_ref.shape
    if begin == 0:
        across = lax.broadcasted_iota(jnp.int32, (width, half), 1) + core_ref[0] * half
        down = lax.broadcasted_iota(jnp.int32, (width, half), 0)
        out_ref[...] = jnp.where(across == down, 1.0, 0.0).astype(F32)
    else:
        out_ref[...] = refs[0][...]
    end = pattern_ref.shape[0] - 2 - 2 * begin

    def step(i, _):
        p = pattern_ref[end - 2 * i] + 2 * pattern_ref[end - 2 * i + 1]

        @pl.when(p < 4)
        def _():
            high, low = split(out_ref[...])
            out_ref[...] += dot(pair_ref[p, 0], high) + dot(pair_ref[p, 1], high) + dot(pair_ref[p, 0], low)

        return 0

    lax.fori_loop(0, count, step, 0)


def join_kernel(core_ref, valid_ref, far_ref, far_other_ref, near_ref, near_other_ref, out_ref, out_other_ref):
    half = near_ref.shape[1]
    total, total_other = jnp.zeros(out_ref.shape, F32), jnp.zeros(out_ref.shape, F32)
    for side, part_ref in ((core_ref[0], far_ref), (1 - core_ref[0], far_other_ref)):
        rows = pl.ds(pl.multiple_of(side * half, half), half)
        part = part_ref[...]
        part_high, part_low = split(jnp.where(valid_ref[0] > 0, part, jnp.zeros_like(part)))

        def times(ref):
            high, low = split(ref[rows, :])
            return dot(part_high, high) + dot(part_low, high) + dot(part_high, low)

        total, total_other = total + times(near_ref), total_other + times(near_other_ref)
    out_ref[...], out_other_ref[...] = total, total_other


def square(ref):
    high, low = split(ref[...])
    ref[...] = 2.0 * ref[...] + dot(high, high) + dot(low, high) + dot(high, low)


def powers_kernel(place_ref, *refs):
    pieces = refs[:8]
    fh_ref, fl_ref, gh_ref, gl_ref, g4h_ref, g4l_ref, kh_ref, kl_ref, now_ref = refs[8:]

    def write(rows, piece, eye):
        now_ref[rows, :] = piece[...] - eye

    gathered(place_ref, pieces, write)
    high, low = split(now_ref[...])
    gh_ref[...], gl_ref[...] = high, low
    product = dot(fh_ref[0], high) + dot(fl_ref[0], high) + dot(fh_ref[0], low)
    both = fh_ref[0].astype(F32) + fl_ref[0].astype(F32) + now_ref[...]
    kh_ref[...], kl_ref[...] = split(product + both)
    square(now_ref)
    square(now_ref)
    g4h_ref[...], g4l_ref[...] = split(now_ref[...])


def middle_kernel(now_ref, p1_ref, p2_ref):
    p1_ref[...] = now_ref[...]
    square(p1_ref)
    square(p1_ref)
    p2_ref[...] = p1_ref[...]
    square(p2_ref)


def far_kernel(p2_ref, p4_ref, p8_ref, p16_ref):
    p4_ref[...] = p2_ref[...]
    square(p4_ref)
    p8_ref[...] = p4_ref[...]
    square(p8_ref)
    p16_ref[...] = p8_ref[...]
    square(p16_ref)


def forward_kernel(mask_ref, final_ref, start_ref, drive_ref, input_ref, pair_ref, bh_ref, bl_ref, gh_ref, gl_ref,
                   g4h_ref, g4l_ref, kh_ref, kl_ref, filtered_ref, gap_ref, part_ref, back_ref, virtual_ref):
    steps, trials, width = drive_ref.shape
    groups, inner = gap_ref.shape[:2]

    def step(i, mean):
        p = mask_ref[2 * i] + 2 * mask_ref[2 * i + 1]
        mean = mean + dot3(mean, pair_ref[p, 0], pair_ref[p, 1]) + input_ref[i]
        filtered_ref[2 * i + 1] = mean
        return mean

    last = lax.fori_loop(0, steps // 2, step, start_ref[...])
    for start in range(0, steps, 8):
        some = range(start, start + 8, 2)
        rows = [start_ref[...] if t == 0 else filtered_ref[t - 1] for t in some]
        moved = chosen_step(jnp.concatenate(rows, 0), [mask_ref[t] for t in some], bh_ref, bl_ref)
        for t, row, part in zip(some, rows, moved):
            filtered_ref[t] = row + part + drive_ref[t]
    virtual = last + dot3(last, bh_ref[0], bl_ref[0])
    virtual_ref[...] = virtual
    for g in range(groups):
        flat = filtered_ref[g * inner : (g + 1) * inner].reshape(inner * trials, width)
        gap_ref[g] = -dot3(flat, kh_ref[...], kl_ref[...]).reshape(inner, trials, width)
    value = gap_ref[:, inner - 1].reshape(groups * trials, width)
    for j in range(inner - 2, -1, -1):
        value = value + dot3(value, gh_ref[...], gl_ref[...]) + gap_ref[:, j].reshape(groups * trials, width)
    part = value.reshape(groups, trials, width)
    part_ref[...] = part
    carry = jnp.where(final_ref[0] > 0, virtual, jnp.zeros_like(virtual))
    for g in range(groups - 1, -1, -1):
        carry = carry + dot3(carry, g4h_ref[...], g4l_ref[...]) + part[g]
    back_ref[...] = carry


def backward_kernel(start_ref, gap_ref, part_ref, gh_ref, gl_ref, g4h_ref, g4l_ref, out_ref):
    groups, inner, trials, width = gap_ref.shape
    carry = start_ref[...]
    starts = [carry]
    for g in range(groups - 1, 0, -1):
        carry = carry + dot3(carry, g4h_ref[...], g4l_ref[...]) + part_ref[g]
        starts.insert(0, carry)
    value = jnp.concatenate(starts, 0)
    for j in range(inner - 1, -1, -1):
        value = value + dot3(value, gh_ref[...], gl_ref[...]) + gap_ref[:, j].reshape(groups * trials, width)
        out_ref[:, j] = value.reshape(groups, trials, width)


def high_dot(left, right):
    return jnp.dot(left, right, precision=lax.Precision.HIGH, preferred_element_type=F32)


def local(observations, mask, transition, updated_transition, smoother_gain, obs_gain, initial_mean):
    steps, trials, channels = observations.shape
    width, panel = transition.shape
    count = lax.axis_size("tm")
    chips = lax.axis_size("state") // 2
    block = lax.axis_index("tm")
    place = lax.axis_index("state")
    chip, core = place // 2, place % 2

    def along_x(a, k):
        return lax.ppermute(
            a, "state", [(2 * i + c, 2 * ((i + k) % chips) + c) for i in range(chips) for c in range(2)]
        )

    def swap(a):
        return lax.ppermute(a, "state", [(2 * i + c, 2 * i + 1 - c) for i in range(chips) for c in range(2)])

    def shifted(a, k):
        return lax.ppermute(a, "tm", [(i, (i + k) % count) for i in range(count)])

    def pieces(own):
        mine = [own] + [along_x(own, k) for k in (1, 2, 3)]
        return mine, [swap(a) for a in mine]

    own, flags = lax.optimization_barrier((jnp.stack([transition.T, updated_transition.T]), mask))
    mine, theirs = pieces(own)
    pattern = jnp.concatenate([jnp.where(block >= k, shifted(flags, k), 2) for k in (2, 1)])
    pattern = jnp.concatenate([jnp.where(block >= 2, shifted(pattern, 2), 2), pattern])
    sources = jnp.stack([(chip - k) % chips for k in range(4)])
    places = jnp.concatenate([2 * sources + core, 2 * sources + 1 - core]).astype(jnp.int32)

    drive = call(
        drive_kernel,
        shape(steps, trials, width),
        [SMEM, VMEM, VMEM],
        (mask, observations.reshape(steps * trials, channels), obs_gain),
        "drive",
        2,
    )

    start = jnp.where(block == 0, initial_mean, jnp.zeros_like(initial_mean))
    bf = functools.partial(shape, width, width, dtype=BF16)
    two = shape(2, width, width, dtype=BF16)
    pattern, places = lax.optimization_barrier((pattern, places))
    last, inputs, bh, bl, pair = call(
        local_kernel,
        (shape(trials, width), shape(steps // 2, trials, width), two, two, shape(4, 2, width, width, dtype=BF16)),
        [SMEM, SMEM] + [VMEM] * 10,
        (places, mask, *mine, *theirs, drive, start),
        "local",
        9,
    )

    half = width // 2
    cores = core.reshape(1).astype(jnp.int32)

    def window(begin, count, *first):
        return call(
            functools.partial(window_kernel, begin, count),
            shape(width, half),
            [SMEM, SMEM, VMEM] + [VMEM] * len(first),
            (cores, pattern, pair, *first),
            f"window{begin + count}",
            0.6 * count,
        )

    def apply(mean, k, mine, theirs):
        mean = jnp.where(block >= k, mean, 0.0)
        here, there = high_dot(mean, mine), high_dot(mean, theirs)
        return jnp.where(
            core == 0, jnp.concatenate([here, there], 1), jnp.concatenate([there, here], 1)
        )

    one, two_back = shifted(last, 1), shifted(last, 2)
    v1 = window(0, 8)
    v1_other = swap(v1)
    v2 = window(8, 8, v1)
    v1, v1_other, v2 = lax.optimization_barrier((v1, v1_other, v2))
    reach = jnp.where(block >= 1, one, 0.0) + apply(two_back, 2, v1, v1_other)

    reach, v2 = lax.optimization_barrier((reach, v2))
    moved = shifted(reach, 2)
    v2_other = swap(v2)
    v4 = window(16, 8, v2)
    v2, v2_other, v4 = lax.optimization_barrier((v2, v2_other, v4))
    reach = reach + apply(moved, 2, v2, v2_other)

    reach, v4 = lax.optimization_barrier((reach, v4))
    moved = shifted(reach, 4)
    v4 = window(24, 8, v4)
    moved, v4 = lax.optimization_barrier((moved, v4))
    v4_far = shifted(v4, 4)
    v4_other = swap(v4)
    reach = reach + apply(moved, 4, v4, v4_other)
    moved = shifted(reach, 8)
    ready, _ = lax.optimization_barrier((smoother_gain.T, reach))
    gain_mine, gain_theirs = pieces(ready)
    gh, gl, g4h, g4l, kh, kl, g4 = call(
        powers_kernel,
        (bf(), bf(), bf(), bf(), bf(), bf(), shape(width, width)),
        [SMEM] + [VMEM] * 10,
        (places, *gain_mine, *gain_theirs, bh, bl),
        "powers",
        4,
    )
    p1, p2 = call(middle_kernel, (shape(width, width),) * 2, [VMEM], (g4,), "middle", 4)
    v4_far, moved, p1, p2 = lax.optimization_barrier((v4_far, moved, p1, p2))
    v8, v8_other = call(
        join_kernel,
        (shape(width, half),) * 2,
        [SMEM, SMEM] + [VMEM] * 4,
        (cores, (block >= 4).reshape(1).astype(jnp.int32), v4_far, swap(v4_far), v4, v4_other),
        "join",
        1.5,
    )
    mean = reach + apply(moved, 8, v8, v8_other)
    for _ in range(2):
        mean = reach + apply(shifted(mean, 8), 8, v8, v8_other)
    mean = jnp.where(block == 0, initial_mean, mean)

    p4, p8, p16 = call(far_kernel, (shape(width, width),) * 3, [VMEM], (p2,), "far", 4)
    far = (p1, p2, p4, p8, p16)

    final = block == count - 1
    filtered, gap, part, back, virtual = call(
        forward_kernel,
        (
            shape(steps, trials, width),
            shape(4, steps // 4, trials, width),
            shape(4, trials, width),
            shape(trials, width),
            shape(trials, width),
        ),
        [SMEM, SMEM] + [VMEM] * 12,
        (mask, final.reshape(1).astype(jnp.int32), mean, drive, inputs, pair, bh, bl, gh, gl, g4h, g4l, kh, kl),
        "forward",
        10,
    )

    scan = lax.all_to_all(back, "tm", 0, 0, tiled=True)
    for k in range(5):
        ahead = jnp.concatenate([scan[2**k :], jnp.zeros((2**k, width), F32)], 0)
        scan = scan + ahead + high_dot(ahead, far[k])
    ahead = jnp.concatenate([scan[1:], jnp.zeros((1, width), F32)], 0)
    back_in = lax.all_to_all(ahead, "tm", 0, 0, tiled=True)
    smoothed = call(
        backward_kernel,
        shape(4, steps // 4, trials, width),
        [VMEM] * 7,
        (jnp.where(final, virtual, back_in), gap, part, gh, gl, g4h, g4l),
        "backward",
        3,
    )
    return filtered, smoothed.reshape(steps, trials, width)


def solution(mesh):
    placed = (
        P("tm", "state", None),
        P("tm"),
        P(None, "state"),
        P(None, "state"),
        P(None, "state"),
        P(),
        P("state", None),
    )
    return jax.shard_map(
        local,
        mesh=mesh,
        in_specs=placed,
        out_specs=(P("tm", "state", None), P("tm", "state", None)),
        check_vma=False,
    )
```

```python
import functools

import jax
import jax.numpy as jnp
from jax import lax
from jax.experimental import pallas as pl
from jax.experimental.pallas import tpu as pltpu
from jax.sharding import PartitionSpec as P

F32 = jnp.float32
BF16 = jnp.bfloat16
VMEM = pl.BlockSpec(memory_space=pltpu.VMEM)
SMEM = pl.BlockSpec(memory_space=pltpu.SMEM)
LIMIT = 16 * 1024 * 1024


def split(a):
    high = a.astype(BF16)
    return high, (a - high.astype(F32)).astype(BF16)


def dot(left, right):
    return jnp.dot(left, right, preferred_element_type=F32)


def dot3(a, high, low):
    rows = a.shape[0]
    a_high, a_low = split(a)
    both = dot(jnp.concatenate([a_high, a_low], 0), high)
    return both[:rows] + both[rows:] + dot(a_high, low)


def call(kernel, outs, specs, args, name, micros, scratch=()):
    return pl.pallas_call(
        kernel,
        out_shape=outs,
        in_specs=specs,
        out_specs=jax.tree.map(lambda _: VMEM, outs),
        scratch_shapes=list(scratch),
        compiler_params=pltpu.CompilerParams(vmem_limit_bytes=LIMIT),
        cost_estimate=pl.CostEstimate(flops=int(micros * 1.15e9), bytes_accessed=1 << 20, transcendentals=0),
        name=name,
    )(*args)


def shape(*dims, dtype=F32):
    return jax.ShapeDtypeStruct(dims, dtype)


def drive_kernel(mask_ref, frames_ref, gain_ref, out_ref):
    high, low = split(gain_ref[...])
    frames = frames_ref[...]
    turned = (((1,), (1,)), ((), ()))
    drive = lax.dot_general(frames, high, turned, preferred_element_type=F32)
    drive = drive + lax.dot_general(frames, low, turned, preferred_element_type=F32)
    steps, trials, _ = out_ref.shape
    for t in range(steps):
        out_ref[t] = drive[t * trials : (t + 1) * trials] * mask_ref[t].astype(F32)


def gathered(place_ref, pieces, write):
    panel, width = pieces[0].shape[-2:]
    for i, piece in enumerate(pieces):
        row = pl.multiple_of(place_ref[i] * panel, panel)
        across = lax.broadcasted_iota(jnp.int32, (panel, width), 1)
        down = lax.broadcasted_iota(jnp.int32, (panel, width), 0) + row
        write(pl.ds(row, panel), piece, jnp.where(across == down, 1.0, 0.0).astype(F32))


def compose(eh, el, lh, ll):
    product = dot(eh, lh) + dot(el, lh) + dot(eh, ll)
    whole = eh.astype(F32) + el.astype(F32) + lh.astype(F32) + ll.astype(F32)
    return split(product + whole)


def chosen_step(rows, flags, high_ref, low_ref):
    parts = [dot3(rows, high_ref[m], low_ref[m]) for m in range(2)]
    size = rows.shape[0] // len(flags)
    return [
        jnp.where(flag > 0, parts[1][i * size : (i + 1) * size], parts[0][i * size : (i + 1) * size])
        for i, flag in enumerate(flags)
    ]


def local_kernel(place_ref, mask_ref, *refs):
    pieces, (drive_ref, start_ref, last_ref, input_ref, high_ref, low_ref, pair_ref) = refs[:8], refs[8:]
    pairs, trials, width = input_ref.shape

    def write(rows, piece, eye):
        for m in range(2):
            high, low = split(piece[m] - eye)
            high_ref[m, rows, :] = high
            low_ref[m, rows, :] = low

    gathered(place_ref, pieces, write)

    def pair(i, _):
        first, second = lax.rem(i, 2), lax.div(i, 2)
        pair_ref[i, 0], pair_ref[i, 1] = compose(high_ref[first], low_ref[first], high_ref[second], low_ref[second])
        return 0

    lax.fori_loop(0, 4, pair, 0)
    for start in range(0, pairs, 4):
        some = range(start, start + 4)
        rows = jnp.concatenate([drive_ref[2 * i] for i in some], 0)
        moved = chosen_step(rows, [mask_ref[2 * i + 1] for i in some], high_ref, low_ref)
        for i, part in zip(some, moved):
            input_ref[i] = drive_ref[2 * i] + part + drive_ref[2 * i + 1]

    def step(i, mean):
        p = mask_ref[2 * i] + 2 * mask_ref[2 * i + 1]
        return mean + dot3(mean, pair_ref[p, 0], pair_ref[p, 1]) + input_ref[i]

    last_ref[...] = lax.fori_loop(0, pairs, step, start_ref[...])


def window_kernel(begin, count, core_ref, pattern_ref, pair_ref, *refs):
    out_ref = refs[-1]
    width, half = out_ref.shape
    if begin == 0:
        across = lax.broadcasted_iota(jnp.int32, (width, half), 1) + core_ref[0] * half
        down = lax.broadcasted_iota(jnp.int32, (width, half), 0)
        out_ref[...] = jnp.where(across == down, 1.0, 0.0).astype(F32)
    else:
        out_ref[...] = refs[0][...]
    end = pattern_ref.shape[0] - 2 - 2 * begin

    def step(i, _):
        p = pattern_ref[end - 2 * i] + 2 * pattern_ref[end - 2 * i + 1]

        @pl.when(p < 4)
        def _():
            high, low = split(out_ref[...])
            out_ref[...] += dot(pair_ref[p, 0], high) + dot(pair_ref[p, 1], high) + dot(pair_ref[p, 0], low)

        return 0

    lax.fori_loop(0, count, step, 0)


def join_kernel(core_ref, valid_ref, far_ref, far_other_ref, near_ref, near_other_ref, out_ref, out_other_ref):
    half = near_ref.shape[1]
    total, total_other = jnp.zeros(out_ref.shape, F32), jnp.zeros(out_ref.shape, F32)
    for side, part_ref in ((core_ref[0], far_ref), (1 - core_ref[0], far_other_ref)):
        rows = pl.ds(pl.multiple_of(side * half, half), half)
        part = part_ref[...]
        part_high, part_low = split(jnp.where(valid_ref[0] > 0, part, jnp.zeros_like(part)))

        def times(ref):
            high, low = split(ref[rows, :])
            return dot(part_high, high) + dot(part_low, high) + dot(part_high, low)

        total, total_other = total + times(near_ref), total_other + times(near_other_ref)
    out_ref[...], out_other_ref[...] = total, total_other


def square(ref):
    high, low = split(ref[...])
    ref[...] = 2.0 * ref[...] + dot(high, high) + dot(low, high) + dot(high, low)


def powers_kernel(place_ref, *refs):
    pieces = refs[:8]
    fh_ref, fl_ref, gh_ref, gl_ref, g4h_ref, g4l_ref, kh_ref, kl_ref, now_ref = refs[8:]

    def write(rows, piece, eye):
        now_ref[rows, :] = piece[...] - eye

    gathered(place_ref, pieces, write)
    high, low = split(now_ref[...])
    gh_ref[...], gl_ref[...] = high, low
    product = dot(fh_ref[0], high) + dot(fl_ref[0], high) + dot(fh_ref[0], low)
    both = fh_ref[0].astype(F32) + fl_ref[0].astype(F32) + now_ref[...]
    kh_ref[...], kl_ref[...] = split(product + both)
    square(now_ref)
    square(now_ref)
    g4h_ref[...], g4l_ref[...] = split(now_ref[...])


def middle_kernel(now_ref, p1_ref, p2_ref):
    p1_ref[...] = now_ref[...]
    square(p1_ref)
    square(p1_ref)
    p2_ref[...] = p1_ref[...]
    square(p2_ref)


def far_kernel(p2_ref, p4_ref, p8_ref, p16_ref):
    p4_ref[...] = p2_ref[...]
    square(p4_ref)
    p8_ref[...] = p4_ref[...]
    square(p8_ref)
    p16_ref[...] = p8_ref[...]
    square(p16_ref)


def forward_kernel(mask_ref, final_ref, start_ref, drive_ref, input_ref, pair_ref, bh_ref, bl_ref, gh_ref, gl_ref,
                   g4h_ref, g4l_ref, kh_ref, kl_ref, filtered_ref, gap_ref, part_ref, back_ref, virtual_ref):
    steps, trials, width = drive_ref.shape
    groups, inner = gap_ref.shape[:2]

    def step(i, mean):
        p = mask_ref[2 * i] + 2 * mask_ref[2 * i + 1]
        mean = mean + dot3(mean, pair_ref[p, 0], pair_ref[p, 1]) + input_ref[i]
        filtered_ref[2 * i + 1] = mean
        return mean

    last = lax.fori_loop(0, steps // 2, step, start_ref[...])
    for start in range(0, steps, 8):
        some = range(start, start + 8, 2)
        rows = [start_ref[...] if t == 0 else filtered_ref[t - 1] for t in some]
        moved = chosen_step(jnp.concatenate(rows, 0), [mask_ref[t] for t in some], bh_ref, bl_ref)
        for t, row, part in zip(some, rows, moved):
            filtered_ref[t] = row + part + drive_ref[t]
    virtual = last + dot3(last, bh_ref[0], bl_ref[0])
    virtual_ref[...] = virtual
    for g in range(groups):
        flat = filtered_ref[g * inner : (g + 1) * inner].reshape(inner * trials, width)
        gap_ref[g] = -dot3(flat, kh_ref[...], kl_ref[...]).reshape(inner, trials, width)
    value = gap_ref[:, inner - 1].reshape(groups * trials, width)
    for j in range(inner - 2, -1, -1):
        value = value + dot3(value, gh_ref[...], gl_ref[...]) + gap_ref[:, j].reshape(groups * trials, width)
    part = value.reshape(groups, trials, width)
    part_ref[...] = part
    carry = jnp.where(final_ref[0] > 0, virtual, jnp.zeros_like(virtual))
    for g in range(groups - 1, -1, -1):
        carry = carry + dot3(carry, g4h_ref[...], g4l_ref[...]) + part[g]
    back_ref[...] = carry


def backward_kernel(start_ref, gap_ref, part_ref, gh_ref, gl_ref, g4h_ref, g4l_ref, out_ref):
    groups, inner, trials, width = gap_ref.shape
    carry = start_ref[...]
    starts = [carry]
    for g in range(groups - 1, 0, -1):
        carry = carry + dot3(carry, g4h_ref[...], g4l_ref[...]) + part_ref[g]
        starts.insert(0, carry)
    value = jnp.concatenate(starts, 0)
    for j in range(inner - 1, -1, -1):
        value = value + dot3(value, gh_ref[...], gl_ref[...]) + gap_ref[:, j].reshape(groups * trials, width)
        out_ref[:, j] = value.reshape(groups, trials, width)


def high_dot(left, right):
    return jnp.dot(left, right, precision=lax.Precision.HIGH, preferred_element_type=F32)


def local(observations, mask, transition, updated_transition, smoother_gain, obs_gain, initial_mean):
    steps, trials, channels = observations.shape
    width, panel = transition.shape
    count = lax.axis_size("tm")
    chips = lax.axis_size("state") // 2
    block = lax.axis_index("tm")
    place = lax.axis_index("state")
    chip, core = place // 2, place % 2

    def along_x(a, k):
        return lax.ppermute(
            a, "state", [(2 * i + c, 2 * ((i + k) % chips) + c) for i in range(chips) for c in range(2)]
        )

    def swap(a):
        return lax.ppermute(a, "state", [(2 * i + c, 2 * i + 1 - c) for i in range(chips) for c in range(2)])

    def shifted(a, k):
        return lax.ppermute(a, "tm", [(i, (i + k) % count) for i in range(count)])

    def pieces(own):
        mine = [own] + [along_x(own, k) for k in (1, 2, 3)]
        return mine, [swap(a) for a in mine]

    own, flags = lax.optimization_barrier((jnp.stack([transition.T, updated_transition.T]), mask))
    mine, theirs = pieces(own)
    pattern = jnp.concatenate([jnp.where(block >= k, shifted(flags, k), 2) for k in (2, 1)])
    pattern = jnp.concatenate([jnp.where(block >= 2, shifted(pattern, 2), 2), pattern])
    sources = jnp.stack([(chip - k) % chips for k in range(4)])
    places = jnp.concatenate([2 * sources + core, 2 * sources + 1 - core]).astype(jnp.int32)

    drive = call(
        drive_kernel,
        shape(steps, trials, width),
        [SMEM, VMEM, VMEM],
        (mask, observations.reshape(steps * trials, channels), obs_gain),
        "drive",
        2,
    )

    start = jnp.where(block == 0, initial_mean, jnp.zeros_like(initial_mean))
    bf = functools.partial(shape, width, width, dtype=BF16)
    two = shape(2, width, width, dtype=BF16)
    pattern, places = lax.optimization_barrier((pattern, places))
    last, inputs, bh, bl, pair = call(
        local_kernel,
        (shape(trials, width), shape(steps // 2, trials, width), two, two, shape(4, 2, width, width, dtype=BF16)),
        [SMEM, SMEM] + [VMEM] * 10,
        (places, mask, *mine, *theirs, drive, start),
        "local",
        9,
    )

    half = width // 2
    cores = core.reshape(1).astype(jnp.int32)

    def window(begin, count, *first):
        return call(
            functools.partial(window_kernel, begin, count),
            shape(width, half),
            [SMEM, SMEM, VMEM] + [VMEM] * len(first),
            (cores, pattern, pair, *first),
            f"window{begin + count}",
            0.6 * count,
        )

    def apply(mean, k, mine, theirs):
        mean = jnp.where(block >= k, mean, 0.0)
        here, there = high_dot(mean, mine), high_dot(mean, theirs)
        return jnp.where(
            core == 0, jnp.concatenate([here, there], 1), jnp.concatenate([there, here], 1)
        )

    one, two_back = shifted(last, 1), shifted(last, 2)
    v1 = window(0, 8)
    v1_other = swap(v1)
    v2 = window(8, 8, v1)
    v1, v1_other, v2 = lax.optimization_barrier((v1, v1_other, v2))
    reach = jnp.where(block >= 1, one, 0.0) + apply(two_back, 2, v1, v1_other)

    reach, v2 = lax.optimization_barrier((reach, v2))
    moved = shifted(reach, 2)
    v2_other = swap(v2)
    v4 = window(16, 8, v2)
    v2, v2_other, v4 = lax.optimization_barrier((v2, v2_other, v4))
    reach = reach + apply(moved, 2, v2, v2_other)

    reach, v4 = lax.optimization_barrier((reach, v4))
    moved = shifted(reach, 4)
    v4 = window(24, 8, v4)
    moved, v4 = lax.optimization_barrier((moved, v4))
    v4_far = shifted(v4, 4)
    v4_other = swap(v4)
    reach = reach + apply(moved, 4, v4, v4_other)
    moved = shifted(reach, 8)
    ready, _ = lax.optimization_barrier((smoother_gain.T, reach))
    gain_mine, gain_theirs = pieces(ready)
    v4_far, moved, *gain = lax.optimization_barrier((v4_far, moved, *gain_mine, *gain_theirs))
    v8, v8_other = call(
        join_kernel,
        (shape(width, half),) * 2,
        [SMEM, SMEM] + [VMEM] * 4,
        (cores, (block >= 4).reshape(1).astype(jnp.int32), v4_far, swap(v4_far), v4, v4_other),
        "join",
        1.5,
    )
    mean = reach + apply(moved, 8, v8, v8_other)
    mean, *gain = lax.optimization_barrier((mean, *gain))
    moved = shifted(mean, 8)
    gh, gl, g4h, g4l, kh, kl, g4 = call(
        powers_kernel,
        (bf(), bf(), bf(), bf(), bf(), bf(), shape(width, width)),
        [SMEM] + [VMEM] * 10,
        (places, *gain, bh, bl),
        "powers",
        12,
    )
    moved, g4 = lax.optimization_barrier((moved, g4))
    mean = reach + apply(moved, 8, v8, v8_other)
    mean, g4 = lax.optimization_barrier((mean, g4))
    moved = shifted(mean, 8)
    p1, p2 = call(middle_kernel, (shape(width, width),) * 2, [VMEM], (g4,), "middle", 12)
    p4, p8, p16 = call(far_kernel, (shape(width, width),) * 3, [VMEM], (p2,), "far", 12)
    moved, p4 = lax.optimization_barrier((moved, p4))
    mean = reach + apply(moved, 8, v8, v8_other)
    mean = jnp.where(block == 0, initial_mean, mean)

    far = (p1, p2, p4, p8, p16)

    final = block == count - 1
    filtered, gap, part, back, virtual = call(
        forward_kernel,
        (
            shape(steps, trials, width),
            shape(4, steps // 4, trials, width),
            shape(4, trials, width),
            shape(trials, width),
            shape(trials, width),
        ),
        [SMEM, SMEM] + [VMEM] * 12,
        (mask, final.reshape(1).astype(jnp.int32), mean, drive, inputs, pair, bh, bl, gh, gl, g4h, g4l, kh, kl),
        "forward",
        10,
    )

    scan = lax.all_to_all(back, "tm", 0, 0, tiled=True)
    for k in range(5):
        ahead = jnp.concatenate([scan[2**k :], jnp.zeros((2**k, width), F32)], 0)
        scan = scan + ahead + high_dot(ahead, far[k])
    ahead = jnp.concatenate([scan[1:], jnp.zeros((1, width), F32)], 0)
    back_in = lax.all_to_all(ahead, "tm", 0, 0, tiled=True)
    smoothed = call(
        backward_kernel,
        shape(4, steps // 4, trials, width),
        [VMEM] * 7,
        (jnp.where(final, virtual, back_in), gap, part, gh, gl, g4h, g4l),
        "backward",
        3,
    )
    return filtered, smoothed.reshape(steps, trials, width)


def solution(mesh):
    placed = (
        P("tm", "state", None),
        P("tm"),
        P(None, "state"),
        P(None, "state"),
        P(None, "state"),
        P(),
        P("state", None),
    )
    return jax.shard_map(
        local,
        mesh=mesh,
        in_specs=placed,
        out_specs=(P("tm", "state", None), P("tm", "state", None)),
        check_vma=False,
    )
```

```python
import functools

import jax
import jax.numpy as jnp
from jax import lax
from jax.experimental import pallas as pl
from jax.experimental.pallas import tpu as pltpu
from jax.sharding import PartitionSpec as P

F32 = jnp.float32
BF16 = jnp.bfloat16
VMEM = pl.BlockSpec(memory_space=pltpu.VMEM)
SMEM = pl.BlockSpec(memory_space=pltpu.SMEM)
LIMIT = 16 * 1024 * 1024


def split(a):
    high = a.astype(BF16)
    return high, (a - high.astype(F32)).astype(BF16)


def dot(left, right):
    return jnp.dot(left, right, preferred_element_type=F32)


def dot3(a, high, low):
    rows = a.shape[0]
    a_high, a_low = split(a)
    both = dot(jnp.concatenate([a_high, a_low], 0), high)
    return both[:rows] + both[rows:] + dot(a_high, low)


def call(kernel, outs, specs, args, name, micros, scratch=()):
    return pl.pallas_call(
        kernel,
        out_shape=outs,
        in_specs=specs,
        out_specs=jax.tree.map(lambda _: VMEM, outs),
        scratch_shapes=list(scratch),
        compiler_params=pltpu.CompilerParams(vmem_limit_bytes=LIMIT),
        cost_estimate=pl.CostEstimate(flops=int(micros * 1.15e9), bytes_accessed=1 << 20, transcendentals=0),
        name=name,
    )(*args)


def shape(*dims, dtype=F32):
    return jax.ShapeDtypeStruct(dims, dtype)


def drive_kernel(mask_ref, frames_ref, gain_ref, out_ref):
    high, low = split(gain_ref[...])
    frames = frames_ref[...]
    turned = (((1,), (1,)), ((), ()))
    drive = lax.dot_general(frames, high, turned, preferred_element_type=F32)
    drive = drive + lax.dot_general(frames, low, turned, preferred_element_type=F32)
    steps, trials, _ = out_ref.shape
    for t in range(steps):
        out_ref[t] = drive[t * trials : (t + 1) * trials] * mask_ref[t].astype(F32)


PIECES = ((0, 0), (1, 0), (2, 0), (3, 0))


def gathered(place_ref, pieces, write):
    width = pieces[0].shape[-1]
    size = pieces[0].shape[-2]
    chips = width // (2 * size)
    place = place_ref[0]
    for i, piece in enumerate(pieces):
        away, first = PIECES[i % len(PIECES)]
        panel = piece.shape[-2]
        core = lax.rem(place + (0 if i < len(PIECES) else 1), 2)
        source = 2 * lax.rem(lax.div(place, 2) + chips - away, chips) + core
        row = pl.multiple_of(source * size + first, panel)
        across = lax.broadcasted_iota(jnp.int32, (panel, width), 1)
        down = lax.broadcasted_iota(jnp.int32, (panel, width), 0) + row
        write(pl.ds(row, panel), piece, jnp.where(across == down, 1.0, 0.0).astype(F32))


def compose(eh, el, lh, ll):
    product = dot(eh, lh) + dot(el, lh) + dot(eh, ll)
    whole = eh.astype(F32) + el.astype(F32) + lh.astype(F32) + ll.astype(F32)
    return split(product + whole)


def chosen_step(rows, flags, high_ref, low_ref):
    parts = [dot3(rows, high_ref[m], low_ref[m]) for m in range(2)]
    size = rows.shape[0] // len(flags)
    return [
        jnp.where(flag > 0, parts[1][i * size : (i + 1) * size], parts[0][i * size : (i + 1) * size])
        for i, flag in enumerate(flags)
    ]


def local_kernel(place_ref, mask_ref, *refs):
    pieces, (drive_ref, start_ref, last_ref, input_ref, high_ref, low_ref, pair_ref) = refs[:8], refs[8:]
    pairs, trials, width = input_ref.shape

    def write(rows, piece, eye):
        for m in range(2):
            high, low = split(piece[m] - eye)
            high_ref[m, rows, :] = high
            low_ref[m, rows, :] = low

    gathered(place_ref, pieces, write)

    def pair(i, _):
        first, second = lax.rem(i, 2), lax.div(i, 2)
        pair_ref[i, 0], pair_ref[i, 1] = compose(high_ref[first], low_ref[first], high_ref[second], low_ref[second])
        return 0

    lax.fori_loop(0, 4, pair, 0)
    for start in range(0, pairs, 4):
        some = range(start, start + 4)
        rows = jnp.concatenate([drive_ref[2 * i] for i in some], 0)
        moved = chosen_step(rows, [mask_ref[2 * i + 1] for i in some], high_ref, low_ref)
        for i, part in zip(some, moved):
            input_ref[i] = drive_ref[2 * i] + part + drive_ref[2 * i + 1]

    def step(i, mean):
        p = mask_ref[2 * i] + 2 * mask_ref[2 * i + 1]
        return mean + dot3(mean, pair_ref[p, 0], pair_ref[p, 1]) + input_ref[i]

    last_ref[...] = lax.fori_loop(0, pairs, step, start_ref[...])


def window_kernel(begin, count, core_ref, pattern_ref, pair_ref, *refs):
    out_ref = refs[-1]
    width, half = out_ref.shape
    if begin == 0:
        across = lax.broadcasted_iota(jnp.int32, (width, half), 1) + core_ref[0] * half
        down = lax.broadcasted_iota(jnp.int32, (width, half), 0)
        out_ref[...] = jnp.where(across == down, 1.0, 0.0).astype(F32)
    else:
        out_ref[...] = refs[0][...]
    end = pattern_ref.shape[0] - 2 - 2 * begin

    def step(i, _):
        p = pattern_ref[end - 2 * i] + 2 * pattern_ref[end - 2 * i + 1]

        @pl.when(p < 4)
        def _():
            high, low = split(out_ref[...])
            out_ref[...] += dot(pair_ref[p, 0], high) + dot(pair_ref[p, 1], high) + dot(pair_ref[p, 0], low)

        return 0

    lax.fori_loop(0, count, step, 0)


def join_kernel(core_ref, valid_ref, far_ref, far_other_ref, near_ref, near_other_ref, out_ref, out_other_ref):
    half = near_ref.shape[1]
    total, total_other = jnp.zeros(out_ref.shape, F32), jnp.zeros(out_ref.shape, F32)
    for side, part_ref in ((core_ref[0], far_ref), (1 - core_ref[0], far_other_ref)):
        rows = pl.ds(pl.multiple_of(side * half, half), half)
        part = part_ref[...]
        part_high, part_low = split(jnp.where(valid_ref[0] > 0, part, jnp.zeros_like(part)))

        def times(ref):
            high, low = split(ref[rows, :])
            return dot(part_high, high) + dot(part_low, high) + dot(part_high, low)

        total, total_other = total + times(near_ref), total_other + times(near_other_ref)
    out_ref[...], out_other_ref[...] = total, total_other


def square(ref):
    high, low = split(ref[...])
    ref[...] = 2.0 * ref[...] + dot(high, high) + dot(low, high) + dot(high, low)


def powers_kernel(place_ref, *refs):
    pieces = refs[:8]
    fh_ref, fl_ref, gh_ref, gl_ref, g4h_ref, g4l_ref, kh_ref, kl_ref, now_ref = refs[8:]

    def write(rows, piece, eye):
        now_ref[rows, :] = piece[...] - eye

    gathered(place_ref, pieces, write)
    high, low = split(now_ref[...])
    gh_ref[...], gl_ref[...] = high, low
    product = dot(fh_ref[0], high) + dot(fl_ref[0], high) + dot(fh_ref[0], low)
    both = fh_ref[0].astype(F32) + fl_ref[0].astype(F32) + now_ref[...]
    kh_ref[...], kl_ref[...] = split(product + both)
    square(now_ref)
    square(now_ref)
    g4h_ref[...], g4l_ref[...] = split(now_ref[...])


def middle_kernel(now_ref, p1_ref, p2_ref):
    p1_ref[...] = now_ref[...]
    square(p1_ref)
    square(p1_ref)
    p2_ref[...] = p1_ref[...]
    square(p2_ref)


def far_kernel(p2_ref, p4_ref, p8_ref, p16_ref):
    p4_ref[...] = p2_ref[...]
    square(p4_ref)
    p8_ref[...] = p4_ref[...]
    square(p8_ref)
    p16_ref[...] = p8_ref[...]
    square(p16_ref)


def forward_kernel(mask_ref, final_ref, start_ref, drive_ref, input_ref, pair_ref, bh_ref, bl_ref, gh_ref, gl_ref,
                   g4h_ref, g4l_ref, kh_ref, kl_ref, filtered_ref, gap_ref, part_ref, back_ref, virtual_ref):
    steps, trials, width = drive_ref.shape
    groups, inner = gap_ref.shape[:2]

    def step(i, mean):
        p = mask_ref[2 * i] + 2 * mask_ref[2 * i + 1]
        mean = mean + dot3(mean, pair_ref[p, 0], pair_ref[p, 1]) + input_ref[i]
        filtered_ref[2 * i + 1] = mean
        return mean

    last = lax.fori_loop(0, steps // 2, step, start_ref[...])
    for start in range(0, steps, 8):
        some = range(start, start + 8, 2)
        rows = [start_ref[...] if t == 0 else filtered_ref[t - 1] for t in some]
        moved = chosen_step(jnp.concatenate(rows, 0), [mask_ref[t] for t in some], bh_ref, bl_ref)
        for t, row, part in zip(some, rows, moved):
            filtered_ref[t] = row + part + drive_ref[t]
    virtual = last + dot3(last, bh_ref[0], bl_ref[0])
    virtual_ref[...] = virtual
    for g in range(groups):
        flat = filtered_ref[g * inner : (g + 1) * inner].reshape(inner * trials, width)
        gap_ref[g] = -dot3(flat, kh_ref[...], kl_ref[...]).reshape(inner, trials, width)
    value = gap_ref[:, inner - 1].reshape(groups * trials, width)
    for j in range(inner - 2, -1, -1):
        value = value + dot3(value, gh_ref[...], gl_ref[...]) + gap_ref[:, j].reshape(groups * trials, width)
    part = value.reshape(groups, trials, width)
    part_ref[...] = part
    carry = jnp.where(final_ref[0] > 0, virtual, jnp.zeros_like(virtual))
    for g in range(groups - 1, -1, -1):
        carry = carry + dot3(carry, g4h_ref[...], g4l_ref[...]) + part[g]
    back_ref[...] = carry


def backward_kernel(start_ref, gap_ref, part_ref, gh_ref, gl_ref, g4h_ref, g4l_ref, out_ref):
    groups, inner, trials, width = gap_ref.shape
    carry = start_ref[...]
    starts = [carry]
    for g in range(groups - 1, 0, -1):
        carry = carry + dot3(carry, g4h_ref[...], g4l_ref[...]) + part_ref[g]
        starts.insert(0, carry)
    value = jnp.concatenate(starts, 0)
    for j in range(inner - 1, -1, -1):
        value = value + dot3(value, gh_ref[...], gl_ref[...]) + gap_ref[:, j].reshape(groups * trials, width)
        out_ref[:, j] = value.reshape(groups, trials, width)


def high_dot(left, right):
    return jnp.dot(left, right, precision=lax.Precision.HIGH, preferred_element_type=F32)


def local(observations, mask, transition, updated_transition, smoother_gain, obs_gain, initial_mean):
    steps, trials, channels = observations.shape
    width, panel = transition.shape
    count = lax.axis_size("tm")
    chips = lax.axis_size("state") // 2
    block = lax.axis_index("tm")
    place = lax.axis_index("state")
    chip, core = place // 2, place % 2

    def along_x(a, k):
        return lax.ppermute(
            a, "state", [(2 * i + c, 2 * ((i + k) % chips) + c) for i in range(chips) for c in range(2)]
        )

    def swap(a):
        return lax.ppermute(a, "state", [(2 * i + c, 2 * i + 1 - c) for i in range(chips) for c in range(2)])

    def shifted(a, k):
        return lax.ppermute(a, "tm", [(i, (i + k) % count) for i in range(count)])

    def along(own):
        return [own] + [along_x(own, k) for k in (1, 2, 3)]

    mine = along(jnp.stack([transition.T, updated_transition.T]))
    theirs = [swap(a) for a in mine]
    places = place.reshape(1).astype(jnp.int32)

    drive = call(
        drive_kernel,
        shape(steps, trials, width),
        [SMEM, VMEM, VMEM],
        (mask, observations.reshape(steps * trials, channels), obs_gain),
        "drive",
        2,
    )

    drive, flags = lax.optimization_barrier((drive, mask))
    pattern = jnp.concatenate([jnp.where(block >= k, shifted(flags, k), 2) for k in (2, 1)])
    pattern = jnp.concatenate([jnp.where(block >= 2, shifted(pattern, 2), 2), pattern])

    start = jnp.where(block == 0, initial_mean, jnp.zeros_like(initial_mean))
    bf = functools.partial(shape, width, width, dtype=BF16)
    two = shape(2, width, width, dtype=BF16)
    last, inputs, bh, bl, pair = call(
        local_kernel,
        (shape(trials, width), shape(steps // 2, trials, width), two, two, shape(4, 2, width, width, dtype=BF16)),
        [SMEM, SMEM] + [VMEM] * 10,
        (places, mask, *mine, *theirs, drive, start),
        "local",
        9,
    )

    half = width // 2
    cores = core.reshape(1).astype(jnp.int32)

    def window(begin, count, *first):
        return call(
            functools.partial(window_kernel, begin, count),
            shape(width, half),
            [SMEM, SMEM, VMEM] + [VMEM] * len(first),
            (cores, pattern, pair, *first),
            f"window{begin + count}",
            0.6 * count,
        )

    def apply(mean, k, mine, theirs):
        mean = jnp.where(block >= k, mean, 0.0)
        here, there = high_dot(mean, mine), high_dot(mean, theirs)
        return jnp.where(
            core == 0, jnp.concatenate([here, there], 1), jnp.concatenate([there, here], 1)
        )

    one, two_back = shifted(last, 1), shifted(last, 2)
    v1 = window(0, 8)
    v1_other = swap(v1)
    v2 = window(8, 8, v1)
    v1, v1_other, v2 = lax.optimization_barrier((v1, v1_other, v2))
    reach = jnp.where(block >= 1, one, 0.0) + apply(two_back, 2, v1, v1_other)

    reach, v2 = lax.optimization_barrier((reach, v2))
    moved = shifted(reach, 2)
    v2_other = swap(v2)
    v4 = window(16, 8, v2)
    v2, v2_other, v4 = lax.optimization_barrier((v2, v2_other, v4))
    reach = reach + apply(moved, 2, v2, v2_other)

    reach, v4 = lax.optimization_barrier((reach, v4))
    moved = shifted(reach, 4)
    v4 = window(24, 8, v4)
    moved, v4 = lax.optimization_barrier((moved, v4))
    v4_far = shifted(v4, 4)
    v4_other = swap(v4)
    reach = reach + apply(moved, 4, v4, v4_other)
    moved = shifted(reach, 8)
    ready, _ = lax.optimization_barrier((smoother_gain.T, reach))
    gain_mine = along(ready)
    v4_far, moved, *gain_mine = lax.optimization_barrier((v4_far, moved, *gain_mine))
    gain = [*gain_mine, *[swap(a) for a in gain_mine]]
    v8, v8_other = call(
        join_kernel,
        (shape(width, half),) * 2,
        [SMEM, SMEM] + [VMEM] * 4,
        (cores, (block >= 4).reshape(1).astype(jnp.int32), v4_far, swap(v4_far), v4, v4_other),
        "join",
        1.5,
    )
    mean = reach + apply(moved, 8, v8, v8_other)
    mean, *gain = lax.optimization_barrier((mean, *gain))
    moved = shifted(mean, 8)
    gh, gl, g4h, g4l, kh, kl, g4 = call(
        powers_kernel,
        (bf(), bf(), bf(), bf(), bf(), bf(), shape(width, width)),
        [SMEM] + [VMEM] * 10,
        (places, *gain, bh, bl),
        "powers",
        12,
    )
    moved, g4 = lax.optimization_barrier((moved, g4))
    mean = reach + apply(moved, 8, v8, v8_other)
    mean, g4 = lax.optimization_barrier((mean, g4))
    moved = shifted(mean, 8)
    p1, p2 = call(middle_kernel, (shape(width, width),) * 2, [VMEM], (g4,), "middle", 12)
    p4, p8, p16 = call(far_kernel, (shape(width, width),) * 3, [VMEM], (p2,), "far", 12)
    moved, p4 = lax.optimization_barrier((moved, p4))
    mean = reach + apply(moved, 8, v8, v8_other)
    mean = jnp.where(block == 0, initial_mean, mean)

    far = (p1, p2, p4, p8, p16)

    final = block == count - 1
    filtered, gap, part, back, virtual = call(
        forward_kernel,
        (
            shape(steps, trials, width),
            shape(4, steps // 4, trials, width),
            shape(4, trials, width),
            shape(trials, width),
            shape(trials, width),
        ),
        [SMEM, SMEM] + [VMEM] * 12,
        (mask, final.reshape(1).astype(jnp.int32), mean, drive, inputs, pair, bh, bl, gh, gl, g4h, g4l, kh, kl),
        "forward",
        10,
    )

    scan = lax.all_to_all(back, "tm", 0, 0, tiled=True)
    for k in range(5):
        ahead = jnp.concatenate([scan[2**k :], jnp.zeros((2**k, width), F32)], 0)
        scan = scan + ahead + high_dot(ahead, far[k])
    ahead = jnp.concatenate([scan[1:], jnp.zeros((1, width), F32)], 0)
    back_in = lax.all_to_all(ahead, "tm", 0, 0, tiled=True)
    smoothed = call(
        backward_kernel,
        shape(4, steps // 4, trials, width),
        [VMEM] * 7,
        (jnp.where(final, virtual, back_in), gap, part, gh, gl, g4h, g4l),
        "backward",
        3,
    )
    return filtered, smoothed.reshape(steps, trials, width)


def solution(mesh):
    placed = (
        P("tm", "state", None),
        P("tm"),
        P(None, "state"),
        P(None, "state"),
        P(None, "state"),
        P(),
        P("state", None),
    )
    return jax.shard_map(
        local,
        mesh=mesh,
        in_specs=placed,
        out_specs=(P("tm", "state", None), P("tm", "state", None)),
        check_vma=False,
    )
```

```python
import functools

import jax
import jax.numpy as jnp
from jax import lax
from jax.experimental import pallas as pl
from jax.experimental.pallas import tpu as pltpu
from jax.sharding import PartitionSpec as P

F32 = jnp.float32
BF16 = jnp.bfloat16
VMEM = pl.BlockSpec(memory_space=pltpu.VMEM)
SMEM = pl.BlockSpec(memory_space=pltpu.SMEM)
LIMIT = 16 * 1024 * 1024


def split(a):
    high = a.astype(BF16)
    return high, (a - high.astype(F32)).astype(BF16)


def dot(left, right):
    return jnp.dot(left, right, preferred_element_type=F32)


def dot3(a, high, low):
    rows = a.shape[0]
    a_high, a_low = split(a)
    both = dot(jnp.concatenate([a_high, a_low], 0), high)
    return both[:rows] + both[rows:] + dot(a_high, low)


def call(kernel, outs, specs, args, name, micros, scratch=()):
    return pl.pallas_call(
        kernel,
        out_shape=outs,
        in_specs=specs,
        out_specs=jax.tree.map(lambda _: VMEM, outs),
        scratch_shapes=list(scratch),
        compiler_params=pltpu.CompilerParams(vmem_limit_bytes=LIMIT),
        cost_estimate=pl.CostEstimate(flops=int(micros * 1.15e9), bytes_accessed=1 << 20, transcendentals=0),
        name=name,
    )(*args)


def shape(*dims, dtype=F32):
    return jax.ShapeDtypeStruct(dims, dtype)


def drive_kernel(mask_ref, frames_ref, gain_ref, out_ref):
    high, low = split(gain_ref[...])
    frames = frames_ref[...]
    turned = (((1,), (1,)), ((), ()))
    drive = lax.dot_general(frames, high, turned, preferred_element_type=F32)
    drive = drive + lax.dot_general(frames, low, turned, preferred_element_type=F32)
    steps, trials, _ = out_ref.shape
    for t in range(steps):
        out_ref[t] = drive[t * trials : (t + 1) * trials] * mask_ref[t].astype(F32)


PIECES = ((0, 0), (1, 0), (2, 0), (3, 0))


def gathered(place_ref, pieces, write):
    width = pieces[0].shape[-1]
    size = pieces[0].shape[-2]
    chips = width // (2 * size)
    place = place_ref[0]
    for i, piece in enumerate(pieces):
        away, first = PIECES[i % len(PIECES)]
        panel = piece.shape[-2]
        core = lax.rem(place + (0 if i < len(PIECES) else 1), 2)
        source = 2 * lax.rem(lax.div(place, 2) + chips - away, chips) + core
        row = pl.multiple_of(source * size + first, panel)
        across = lax.broadcasted_iota(jnp.int32, (panel, width), 1)
        down = lax.broadcasted_iota(jnp.int32, (panel, width), 0) + row
        write(pl.ds(row, panel), piece, jnp.where(across == down, 1.0, 0.0).astype(F32))


def compose(eh, el, lh, ll):
    product = dot(eh, lh) + dot(el, lh) + dot(eh, ll)
    whole = eh.astype(F32) + el.astype(F32) + lh.astype(F32) + ll.astype(F32)
    return split(product + whole)


def chosen_step(rows, flags, high_ref, low_ref):
    parts = [dot3(rows, high_ref[m], low_ref[m]) for m in range(2)]
    size = rows.shape[0] // len(flags)
    return [
        jnp.where(flag > 0, parts[1][i * size : (i + 1) * size], parts[0][i * size : (i + 1) * size])
        for i, flag in enumerate(flags)
    ]


def local_kernel(place_ref, mask_ref, *refs):
    pieces, (drive_ref, start_ref, last_ref, input_ref, high_ref, low_ref, pair_ref) = refs[:8], refs[8:]
    pairs, trials, width = input_ref.shape

    def write(rows, piece, eye):
        for m in range(2):
            high, low = split(piece[m] - eye)
            high_ref[m, rows, :] = high
            low_ref[m, rows, :] = low

    gathered(place_ref, pieces, write)

    def pair(i, _):
        first, second = lax.rem(i, 2), lax.div(i, 2)
        pair_ref[i, 0], pair_ref[i, 1] = compose(high_ref[first], low_ref[first], high_ref[second], low_ref[second])
        return 0

    lax.fori_loop(0, 4, pair, 0)
    for start in range(0, pairs, 4):
        some = range(start, start + 4)
        rows = jnp.concatenate([drive_ref[2 * i] for i in some], 0)
        moved = chosen_step(rows, [mask_ref[2 * i + 1] for i in some], high_ref, low_ref)
        for i, part in zip(some, moved):
            input_ref[i] = drive_ref[2 * i] + part + drive_ref[2 * i + 1]

    def step(i, mean):
        p = mask_ref[2 * i] + 2 * mask_ref[2 * i + 1]
        return mean + dot3(mean, pair_ref[p, 0], pair_ref[p, 1]) + input_ref[i]

    last_ref[...] = lax.fori_loop(0, pairs, step, start_ref[...])


def window_kernel(begin, count, core_ref, pattern_ref, pair_ref, *refs):
    out_ref = refs[-1]
    width, half = out_ref.shape
    if begin == 0:
        across = lax.broadcasted_iota(jnp.int32, (width, half), 1) + core_ref[0] * half
        down = lax.broadcasted_iota(jnp.int32, (width, half), 0)
        out_ref[...] = jnp.where(across == down, 1.0, 0.0).astype(F32)
    else:
        out_ref[...] = refs[0][...]
    end = pattern_ref.shape[0] - 2 - 2 * begin

    def step(i, _):
        p = pattern_ref[end - 2 * i] + 2 * pattern_ref[end - 2 * i + 1]

        @pl.when(p < 4)
        def _():
            high, low = split(out_ref[...])
            out_ref[...] += dot(pair_ref[p, 0], high) + dot(pair_ref[p, 1], high) + dot(pair_ref[p, 0], low)

        return 0

    lax.fori_loop(0, count, step, 0)


def join_kernel(core_ref, valid_ref, far_ref, far_other_ref, near_ref, near_other_ref, out_ref, out_other_ref):
    half = near_ref.shape[1]
    total, total_other = jnp.zeros(out_ref.shape, F32), jnp.zeros(out_ref.shape, F32)
    for side, part_ref in ((core_ref[0], far_ref), (1 - core_ref[0], far_other_ref)):
        rows = pl.ds(pl.multiple_of(side * half, half), half)
        part = part_ref[...]
        part_high, part_low = split(jnp.where(valid_ref[0] > 0, part, jnp.zeros_like(part)))

        def times(ref):
            high, low = split(ref[rows, :])
            return dot(part_high, high) + dot(part_low, high) + dot(part_high, low)

        total, total_other = total + times(near_ref), total_other + times(near_other_ref)
    out_ref[...], out_other_ref[...] = total, total_other


def square(ref):
    high, low = split(ref[...])
    ref[...] = 2.0 * ref[...] + dot(high, high) + dot(low, high) + dot(high, low)


def powers_kernel(place_ref, *refs):
    pieces = refs[:8]
    fh_ref, fl_ref, gh_ref, gl_ref, g4h_ref, g4l_ref, kh_ref, kl_ref, now_ref = refs[8:]

    def write(rows, piece, eye):
        now_ref[rows, :] = piece[...] - eye

    gathered(place_ref, pieces, write)
    high, low = split(now_ref[...])
    gh_ref[...], gl_ref[...] = high, low
    product = dot(fh_ref[0], high) + dot(fl_ref[0], high) + dot(fh_ref[0], low)
    both = fh_ref[0].astype(F32) + fl_ref[0].astype(F32) + now_ref[...]
    kh_ref[...], kl_ref[...] = split(product + both)
    square(now_ref)
    square(now_ref)
    g4h_ref[...], g4l_ref[...] = split(now_ref[...])


def middle_kernel(now_ref, p1_ref, p2_ref):
    p1_ref[...] = now_ref[...]
    square(p1_ref)
    square(p1_ref)
    p2_ref[...] = p1_ref[...]
    square(p2_ref)


def far_kernel(p2_ref, p4_ref, p8_ref, p16_ref):
    p4_ref[...] = p2_ref[...]
    square(p4_ref)
    p8_ref[...] = p4_ref[...]
    square(p8_ref)
    p16_ref[...] = p8_ref[...]
    square(p16_ref)


def forward_kernel(mask_ref, final_ref, start_ref, drive_ref, input_ref, pair_ref, bh_ref, bl_ref, gh_ref, gl_ref,
                   g4h_ref, g4l_ref, kh_ref, kl_ref, filtered_ref, gap_ref, part_ref, back_ref, virtual_ref):
    steps, trials, width = drive_ref.shape
    groups, inner = gap_ref.shape[:2]

    def step(i, mean):
        p = mask_ref[2 * i] + 2 * mask_ref[2 * i + 1]
        mean = mean + dot3(mean, pair_ref[p, 0], pair_ref[p, 1]) + input_ref[i]
        filtered_ref[2 * i + 1] = mean
        return mean

    last = lax.fori_loop(0, steps // 2, step, start_ref[...])
    for start in range(0, steps, 8):
        some = range(start, start + 8, 2)
        rows = [start_ref[...] if t == 0 else filtered_ref[t - 1] for t in some]
        moved = chosen_step(jnp.concatenate(rows, 0), [mask_ref[t] for t in some], bh_ref, bl_ref)
        for t, row, part in zip(some, rows, moved):
            filtered_ref[t] = row + part + drive_ref[t]
    virtual = last + dot3(last, bh_ref[0], bl_ref[0])
    virtual_ref[...] = virtual
    for g in range(groups):
        flat = filtered_ref[g * inner : (g + 1) * inner].reshape(inner * trials, width)
        gap_ref[g] = -dot3(flat, kh_ref[...], kl_ref[...]).reshape(inner, trials, width)
    value = gap_ref[:, inner - 1].reshape(groups * trials, width)
    for j in range(inner - 2, -1, -1):
        value = value + dot3(value, gh_ref[...], gl_ref[...]) + gap_ref[:, j].reshape(groups * trials, width)
    part = value.reshape(groups, trials, width)
    part_ref[...] = part
    carry = jnp.where(final_ref[0] > 0, virtual, jnp.zeros_like(virtual))
    for g in range(groups - 1, -1, -1):
        carry = carry + dot3(carry, g4h_ref[...], g4l_ref[...]) + part[g]
    back_ref[...] = carry


def backward_kernel(start_ref, gap_ref, part_ref, gh_ref, gl_ref, g4h_ref, g4l_ref, out_ref):
    groups, inner, trials, width = gap_ref.shape
    carry = start_ref[...]
    starts = [carry]
    for g in range(groups - 1, 0, -1):
        carry = carry + dot3(carry, g4h_ref[...], g4l_ref[...]) + part_ref[g]
        starts.insert(0, carry)
    value = jnp.concatenate(starts, 0)
    for j in range(inner - 1, -1, -1):
        value = value + dot3(value, gh_ref[...], gl_ref[...]) + gap_ref[:, j].reshape(groups * trials, width)
        out_ref[:, j] = value.reshape(groups, trials, width)


def high_dot(left, right):
    return jnp.dot(left, right, precision=lax.Precision.HIGH, preferred_element_type=F32)


def local(observations, mask, transition, updated_transition, smoother_gain, obs_gain, initial_mean):
    steps, trials, channels = observations.shape
    width, panel = transition.shape
    count = lax.axis_size("tm")
    chips = lax.axis_size("state") // 2
    block = lax.axis_index("tm")
    place = lax.axis_index("state")
    chip, core = place // 2, place % 2

    def along_x(a, k):
        return lax.ppermute(
            a, "state", [(2 * i + c, 2 * ((i + k) % chips) + c) for i in range(chips) for c in range(2)]
        )

    def swap(a):
        return lax.ppermute(a, "state", [(2 * i + c, 2 * i + 1 - c) for i in range(chips) for c in range(2)])

    def shifted(a, k):
        return lax.ppermute(a, "tm", [(i, (i + k) % count) for i in range(count)])

    def along(own):
        return [own] + [along_x(own, k) for k in (1, 2, 3)]

    own = jnp.stack([transition.T, updated_transition.T])
    mine = along(own)
    own, mine[3], gain_own = lax.optimization_barrier((own, mine[3], smoother_gain.T))
    theirs = [swap(a) for a in (own, *mine[1:])]
    gain_mine = along(gain_own)
    places = place.reshape(1).astype(jnp.int32)

    drive = call(
        drive_kernel,
        shape(steps, trials, width),
        [SMEM, VMEM, VMEM],
        (mask, observations.reshape(steps * trials, channels), obs_gain),
        "drive",
        2,
    )

    drive, flags = lax.optimization_barrier((drive, mask))
    recent = jnp.concatenate([jnp.where(block >= k, shifted(flags, k), 2) for k in (2, 1)])
    pattern = jnp.concatenate([jnp.where(block >= 2, shifted(recent, 2), 2), recent])

    start = jnp.where(block == 0, initial_mean, jnp.zeros_like(initial_mean))
    bf = functools.partial(shape, width, width, dtype=BF16)
    two = shape(2, width, width, dtype=BF16)
    last, inputs, bh, bl, pair = call(
        local_kernel,
        (shape(trials, width), shape(steps // 2, trials, width), two, two, shape(4, 2, width, width, dtype=BF16)),
        [SMEM, SMEM] + [VMEM] * 10,
        (places, mask, *mine, *theirs, drive, start),
        "local",
        9,
    )

    pair, *gain_mine = lax.optimization_barrier((pair, *gain_mine))
    half = width // 2
    cores = core.reshape(1).astype(jnp.int32)

    def window(begin, count, pattern, *first):
        return call(
            functools.partial(window_kernel, begin, count),
            shape(width, half),
            [SMEM, SMEM, VMEM] + [VMEM] * len(first),
            (cores, pattern, pair, *first),
            f"window{begin + count}",
            0.6 * count,
        )

    def apply(mean, k, mine, theirs):
        mean = jnp.where(block >= k, mean, 0.0)
        here, there = high_dot(mean, mine), high_dot(mean, theirs)
        return jnp.where(
            core == 0, jnp.concatenate([here, there], 1), jnp.concatenate([there, here], 1)
        )

    one, two_back = shifted(last, 1), shifted(last, 2)
    v1 = window(0, 8, recent)
    v1_other = swap(v1)
    v2 = window(8, 8, recent, v1)
    v1, v1_other, v2 = lax.optimization_barrier((v1, v1_other, v2))
    reach = jnp.where(block >= 1, one, 0.0) + apply(two_back, 2, v1, v1_other)

    reach, v2 = lax.optimization_barrier((reach, v2))
    moved = shifted(reach, 2)
    v2_other = swap(v2)
    v4 = window(16, 8, pattern, v2)
    v2, v2_other, v4 = lax.optimization_barrier((v2, v2_other, v4))
    reach = reach + apply(moved, 2, v2, v2_other)

    reach, v4 = lax.optimization_barrier((reach, v4))
    moved = shifted(reach, 4)
    v4 = window(24, 8, pattern, v4)
    moved, v4 = lax.optimization_barrier((moved, v4))
    v4_far = shifted(v4, 4)
    v4_other = swap(v4)
    gain_theirs = [swap(a) for a in gain_mine]
    reach = reach + apply(moved, 4, v4, v4_other)
    moved = shifted(reach, 8)
    v4_far, moved = lax.optimization_barrier((v4_far, moved))
    v8, v8_other = call(
        join_kernel,
        (shape(width, half),) * 2,
        [SMEM, SMEM] + [VMEM] * 4,
        (cores, (block >= 4).reshape(1).astype(jnp.int32), v4_far, swap(v4_far), v4, v4_other),
        "join",
        1.5,
    )
    mean = reach + apply(moved, 8, v8, v8_other)
    gain_mine[0], mean = lax.optimization_barrier((gain_mine[0], mean))
    gain = [*gain_mine, *gain_theirs]
    moved = shifted(mean, 8)
    gh, gl, g4h, g4l, kh, kl, g4 = call(
        powers_kernel,
        (bf(), bf(), bf(), bf(), bf(), bf(), shape(width, width)),
        [SMEM] + [VMEM] * 10,
        (places, *gain, bh, bl),
        "powers",
        12,
    )
    moved, g4 = lax.optimization_barrier((moved, g4))
    mean = reach + apply(moved, 8, v8, v8_other)
    mean, g4 = lax.optimization_barrier((mean, g4))
    moved = shifted(mean, 8)
    p1, p2 = call(middle_kernel, (shape(width, width),) * 2, [VMEM], (g4,), "middle", 12)
    p4, p8, p16 = call(far_kernel, (shape(width, width),) * 3, [VMEM], (p2,), "far", 12)
    moved, p4 = lax.optimization_barrier((moved, p4))
    mean = reach + apply(moved, 8, v8, v8_other)
    mean = jnp.where(block == 0, initial_mean, mean)

    far = (p1, p2, p4, p8, p16)

    final = block == count - 1
    filtered, gap, part, back, virtual = call(
        forward_kernel,
        (
            shape(steps, trials, width),
            shape(4, steps // 4, trials, width),
            shape(4, trials, width),
            shape(trials, width),
            shape(trials, width),
        ),
        [SMEM, SMEM] + [VMEM] * 12,
        (mask, final.reshape(1).astype(jnp.int32), mean, drive, inputs, pair, bh, bl, gh, gl, g4h, g4l, kh, kl),
        "forward",
        10,
    )

    scan = lax.all_to_all(back, "tm", 0, 0, tiled=True)
    for k in range(5):
        ahead = jnp.concatenate([scan[2**k :], jnp.zeros((2**k, width), F32)], 0)
        scan = scan + ahead + high_dot(ahead, far[k])
    ahead = jnp.concatenate([scan[1:], jnp.zeros((1, width), F32)], 0)
    back_in = lax.all_to_all(ahead, "tm", 0, 0, tiled=True)
    smoothed = call(
        backward_kernel,
        shape(4, steps // 4, trials, width),
        [VMEM] * 7,
        (jnp.where(final, virtual, back_in), gap, part, gh, gl, g4h, g4l),
        "backward",
        3,
    )
    return filtered, smoothed.reshape(steps, trials, width)


def solution(mesh):
    placed = (
        P("tm", "state", None),
        P("tm"),
        P(None, "state"),
        P(None, "state"),
        P(None, "state"),
        P(),
        P("state", None),
    )
    return jax.shard_map(
        local,
        mesh=mesh,
        in_specs=placed,
        out_specs=(P("tm", "state", None), P("tm", "state", None)),
        check_vma=False,
    )
```

```python
import functools

import jax
import jax.numpy as jnp
from jax import lax
from jax.experimental import pallas as pl
from jax.experimental.pallas import tpu as pltpu
from jax.sharding import PartitionSpec as P

F32 = jnp.float32
BF16 = jnp.bfloat16
VMEM = pl.BlockSpec(memory_space=pltpu.VMEM)
SMEM = pl.BlockSpec(memory_space=pltpu.SMEM)
LIMIT = 16 * 1024 * 1024


def split(a):
    high = a.astype(BF16)
    return high, (a - high.astype(F32)).astype(BF16)


def dot(left, right):
    return jnp.dot(left, right, preferred_element_type=F32)


def dot3(a, high, low):
    rows = a.shape[0]
    a_high, a_low = split(a)
    both = dot(jnp.concatenate([a_high, a_low], 0), high)
    return both[:rows] + both[rows:] + dot(a_high, low)


def call(kernel, outs, specs, args, name, micros, scratch=(), out_specs=None):
    return pl.pallas_call(
        kernel,
        out_shape=outs,
        in_specs=specs,
        out_specs=jax.tree.map(lambda _: VMEM, outs) if out_specs is None else out_specs,
        scratch_shapes=list(scratch),
        compiler_params=pltpu.CompilerParams(vmem_limit_bytes=LIMIT),
        cost_estimate=pl.CostEstimate(flops=int(micros * 1.15e9), bytes_accessed=1 << 20, transcendentals=0),
        name=name,
    )(*args)


def shape(*dims, dtype=F32):
    return jax.ShapeDtypeStruct(dims, dtype)


def drive_kernel(mask_ref, frames_ref, gain_ref, out_ref, flags_ref):
    high, low = split(gain_ref[...])
    frames = frames_ref[...]
    turned = (((1,), (1,)), ((), ()))
    drive = lax.dot_general(frames, high, turned, preferred_element_type=F32)
    drive = drive + lax.dot_general(frames, low, turned, preferred_element_type=F32)
    steps, trials, _ = out_ref.shape
    for t in range(steps):
        out_ref[t] = drive[t * trials : (t + 1) * trials] * mask_ref[t].astype(F32)
        flags_ref[t] = mask_ref[t]


PIECES = ((0, 0), (1, 0), (2, 0), (3, 0))


def gathered(place_ref, pieces, write):
    width = pieces[0].shape[-1]
    size = pieces[0].shape[-2]
    chips = width // (2 * size)
    place = place_ref[0]
    for i, piece in enumerate(pieces):
        away, first = PIECES[i % len(PIECES)]
        panel = piece.shape[-2]
        core = lax.rem(place + (0 if i < len(PIECES) else 1), 2)
        source = 2 * lax.rem(lax.div(place, 2) + chips - away, chips) + core
        row = pl.multiple_of(source * size + first, panel)
        across = lax.broadcasted_iota(jnp.int32, (panel, width), 1)
        down = lax.broadcasted_iota(jnp.int32, (panel, width), 0) + row
        write(pl.ds(row, panel), piece, jnp.where(across == down, 1.0, 0.0).astype(F32))


def gain_kernel(place_ref, own_ref, out_ref):
    panel, width = own_ref.shape
    across = lax.broadcasted_iota(jnp.int32, (panel, width), 1)
    down = lax.broadcasted_iota(jnp.int32, (panel, width), 0) + place_ref[0] * panel
    out_ref[...] = own_ref[...] - jnp.where(across == down, 1.0, 0.0).astype(F32)


def compose(eh, el, lh, ll):
    product = dot(eh, lh) + dot(el, lh) + dot(eh, ll)
    whole = eh.astype(F32) + el.astype(F32) + lh.astype(F32) + ll.astype(F32)
    return split(product + whole)


def chosen_step(rows, flags, high_ref, low_ref):
    parts = [dot3(rows, high_ref[m], low_ref[m]) for m in range(2)]
    size = rows.shape[0] // len(flags)
    return [
        jnp.where(flag > 0, parts[1][i * size : (i + 1) * size], parts[0][i * size : (i + 1) * size])
        for i, flag in enumerate(flags)
    ]


def local_kernel(place_ref, mask_ref, *refs):
    pieces, (drive_ref, start_ref, last_ref, input_ref, high_ref, low_ref, pair_ref) = refs[:8], refs[8:]
    pairs, trials, width = input_ref.shape

    def write(rows, piece, eye):
        for m in range(2):
            high, low = split(piece[m] - eye)
            high_ref[m, rows, :] = high
            low_ref[m, rows, :] = low

    gathered(place_ref, pieces, write)

    def pair(i, _):
        first, second = lax.rem(i, 2), lax.div(i, 2)
        pair_ref[i, 0], pair_ref[i, 1] = compose(high_ref[first], low_ref[first], high_ref[second], low_ref[second])
        return 0

    lax.fori_loop(0, 4, pair, 0)
    for start in range(0, pairs, 4):
        some = range(start, start + 4)
        rows = jnp.concatenate([drive_ref[2 * i] for i in some], 0)
        moved = chosen_step(rows, [mask_ref[2 * i + 1] for i in some], high_ref, low_ref)
        for i, part in zip(some, moved):
            input_ref[i] = drive_ref[2 * i] + part + drive_ref[2 * i + 1]

    def step(i, mean):
        p = mask_ref[2 * i] + 2 * mask_ref[2 * i + 1]
        return mean + dot3(mean, pair_ref[p, 0], pair_ref[p, 1]) + input_ref[i]

    last_ref[...] = lax.fori_loop(0, pairs, step, start_ref[...])


def window_kernel(begin, count, core_ref, pattern_ref, pair_ref, *refs):
    out_ref = refs[-1]
    width, half = out_ref.shape
    if begin == 0:
        across = lax.broadcasted_iota(jnp.int32, (width, half), 1) + core_ref[0] * half
        down = lax.broadcasted_iota(jnp.int32, (width, half), 0)
        out_ref[...] = jnp.where(across == down, 1.0, 0.0).astype(F32)
    else:
        out_ref[...] = refs[0][...]
    end = pattern_ref.shape[0] - 2 - 2 * begin

    def step(i, _):
        p = pattern_ref[end - 2 * i] + 2 * pattern_ref[end - 2 * i + 1]

        @pl.when(p < 4)
        def _():
            high, low = split(out_ref[...])
            out_ref[...] += dot(pair_ref[p, 0], high) + dot(pair_ref[p, 1], high) + dot(pair_ref[p, 0], low)

        return 0

    lax.fori_loop(0, count, step, 0)


def join_kernel(core_ref, valid_ref, far_ref, far_other_ref, near_ref, near_other_ref, out_ref, out_other_ref):
    half = near_ref.shape[1]
    total, total_other = jnp.zeros(out_ref.shape, F32), jnp.zeros(out_ref.shape, F32)
    for side, part_ref in ((core_ref[0], far_ref), (1 - core_ref[0], far_other_ref)):
        rows = pl.ds(pl.multiple_of(side * half, half), half)
        part = part_ref[...]
        part_high, part_low = split(jnp.where(valid_ref[0] > 0, part, jnp.zeros_like(part)))

        def times(ref):
            high, low = split(ref[rows, :])
            return dot(part_high, high) + dot(part_low, high) + dot(part_high, low)

        total, total_other = total + times(near_ref), total_other + times(near_other_ref)
    out_ref[...], out_other_ref[...] = total, total_other


def square(ref):
    high, low = split(ref[...])
    ref[...] = 2.0 * ref[...] + dot(high, high) + dot(low, high) + dot(high, low)


def powers_kernel(place_ref, *refs):
    pieces = refs[:8]
    fh_ref, fl_ref, gh_ref, gl_ref, g4h_ref, g4l_ref, kh_ref, kl_ref, now_ref = refs[8:]

    def write(rows, piece, _):
        now_ref[rows, :] = piece[...]

    gathered(place_ref, pieces, write)
    high, low = split(now_ref[...])
    gh_ref[...], gl_ref[...] = high, low
    product = dot(fh_ref[0], high) + dot(fl_ref[0], high) + dot(fh_ref[0], low)
    both = fh_ref[0].astype(F32) + fl_ref[0].astype(F32) + now_ref[...]
    kh_ref[...], kl_ref[...] = split(product + both)
    square(now_ref)
    square(now_ref)
    g4h_ref[...], g4l_ref[...] = split(now_ref[...])


def middle_kernel(now_ref, p1_ref, p2_ref):
    p1_ref[...] = now_ref[...]
    square(p1_ref)
    square(p1_ref)
    p2_ref[...] = p1_ref[...]
    square(p2_ref)


def far_kernel(p2_ref, p4_ref, p8_ref, p16_ref):
    p4_ref[...] = p2_ref[...]
    square(p4_ref)
    p8_ref[...] = p4_ref[...]
    square(p8_ref)
    p16_ref[...] = p8_ref[...]
    square(p16_ref)


def forward_kernel(mask_ref, final_ref, start_ref, drive_ref, input_ref, pair_ref, bh_ref, bl_ref, gh_ref, gl_ref,
                   g4h_ref, g4l_ref, kh_ref, kl_ref, filtered_ref, gap_ref, part_ref, back_ref, virtual_ref):
    steps, trials, width = drive_ref.shape
    groups, inner = gap_ref.shape[:2]

    def step(i, mean):
        p = mask_ref[2 * i] + 2 * mask_ref[2 * i + 1]
        mean = mean + dot3(mean, pair_ref[p, 0], pair_ref[p, 1]) + input_ref[i]
        filtered_ref[2 * i + 1] = mean
        return mean

    last = lax.fori_loop(0, steps // 2, step, start_ref[...])
    for start in range(0, steps, 8):
        some = range(start, start + 8, 2)
        rows = [start_ref[...] if t == 0 else filtered_ref[t - 1] for t in some]
        moved = chosen_step(jnp.concatenate(rows, 0), [mask_ref[t] for t in some], bh_ref, bl_ref)
        for t, row, part in zip(some, rows, moved):
            filtered_ref[t] = row + part + drive_ref[t]
    virtual = last + dot3(last, bh_ref[0], bl_ref[0])
    virtual_ref[...] = virtual
    for g in range(groups):
        flat = filtered_ref[g * inner : (g + 1) * inner].reshape(inner * trials, width)
        gap_ref[g] = -dot3(flat, kh_ref[...], kl_ref[...]).reshape(inner, trials, width)
    value = gap_ref[:, inner - 1].reshape(groups * trials, width)
    for j in range(inner - 2, -1, -1):
        value = value + dot3(value, gh_ref[...], gl_ref[...]) + gap_ref[:, j].reshape(groups * trials, width)
    part = value.reshape(groups, trials, width)
    part_ref[...] = part
    carry = jnp.where(final_ref[0] > 0, virtual, jnp.zeros_like(virtual))
    for g in range(groups - 1, -1, -1):
        carry = carry + dot3(carry, g4h_ref[...], g4l_ref[...]) + part[g]
    back_ref[...] = carry


def backward_kernel(start_ref, gap_ref, part_ref, gh_ref, gl_ref, g4h_ref, g4l_ref, out_ref):
    groups, inner, trials, width = gap_ref.shape
    carry = start_ref[...]
    starts = [carry]
    for g in range(groups - 1, 0, -1):
        carry = carry + dot3(carry, g4h_ref[...], g4l_ref[...]) + part_ref[g]
        starts.insert(0, carry)
    value = jnp.concatenate(starts, 0)
    for j in range(inner - 1, -1, -1):
        value = value + dot3(value, gh_ref[...], gl_ref[...]) + gap_ref[:, j].reshape(groups * trials, width)
        out_ref[:, j] = value.reshape(groups, trials, width)


def high_dot(left, right):
    return jnp.dot(left, right, precision=lax.Precision.HIGH, preferred_element_type=F32)


def local(observations, mask, transition, updated_transition, smoother_gain, obs_gain, initial_mean):
    steps, trials, channels = observations.shape
    width, panel = transition.shape
    count = lax.axis_size("tm")
    chips = lax.axis_size("state") // 2
    block = lax.axis_index("tm")
    place = lax.axis_index("state")
    chip, core = place // 2, place % 2

    def along_x(a, k):
        return lax.ppermute(
            a, "state", [(2 * i + c, 2 * ((i + k) % chips) + c) for i in range(chips) for c in range(2)]
        )

    def swap(a):
        return lax.ppermute(a, "state", [(2 * i + c, 2 * i + 1 - c) for i in range(chips) for c in range(2)])

    def shifted(a, k):
        return lax.ppermute(a, "tm", [(i, (i + k) % count) for i in range(count)])

    def along(own):
        return [own] + [along_x(own, k) for k in (1, 2, 3)]

    own = jnp.stack([transition.T, updated_transition.T])
    mine = along(own)
    own, mine[3] = lax.optimization_barrier((own, mine[3]))
    theirs = [swap(a) for a in (own, *mine[1:])]
    places = place.reshape(1).astype(jnp.int32)

    drive, flags = call(
        drive_kernel,
        (shape(steps, trials, width), shape(steps, dtype=jnp.int32)),
        [SMEM, VMEM, VMEM],
        (mask, observations.reshape(steps * trials, channels), obs_gain),
        "drive",
        2,
        out_specs=(VMEM, SMEM),
    )
    recent = jnp.concatenate([jnp.where(block >= k, shifted(flags, k), 2) for k in (2, 1)])
    pattern = jnp.concatenate([jnp.where(block >= 2, shifted(recent, 2), 2), recent])

    start = jnp.where(block == 0, initial_mean, jnp.zeros_like(initial_mean))
    bf = functools.partial(shape, width, width, dtype=BF16)
    two = shape(2, width, width, dtype=BF16)
    last, inputs, bh, bl, pair = call(
        local_kernel,
        (shape(trials, width), shape(steps // 2, trials, width), two, two, shape(4, 2, width, width, dtype=BF16)),
        [SMEM, SMEM] + [VMEM] * 10,
        (places, mask, *mine, *theirs, drive, start),
        "local",
        9,
    )

    half = width // 2
    cores = core.reshape(1).astype(jnp.int32)

    def window(begin, count, pattern, *first):
        return call(
            functools.partial(window_kernel, begin, count),
            shape(width, half),
            [SMEM, SMEM, VMEM] + [VMEM] * len(first),
            (cores, pattern, pair, *first),
            f"window{begin + count}",
            0.6 * count,
        )

    def apply(mean, k, mine, theirs):
        mean = jnp.where(block >= k, mean, 0.0)
        here, there = high_dot(mean, mine), high_dot(mean, theirs)
        return jnp.where(
            core == 0, jnp.concatenate([here, there], 1), jnp.concatenate([there, here], 1)
        )

    one, two_back = shifted(last, 1), shifted(last, 2)
    v1 = window(0, 8, recent)
    v1_other = swap(v1)
    v2 = window(8, 8, recent, v1)
    v1, v1_other, v2 = lax.optimization_barrier((v1, v1_other, v2))
    reach = jnp.where(block >= 1, one, 0.0) + apply(two_back, 2, v1, v1_other)

    reach, v2 = lax.optimization_barrier((reach, v2))
    moved = shifted(reach, 2)
    v2_other = swap(v2)
    v4 = window(16, 8, pattern, v2)
    v2, v2_other, v4 = lax.optimization_barrier((v2, v2_other, v4))
    reach = reach + apply(moved, 2, v2, v2_other)

    reach, v4 = lax.optimization_barrier((reach, v4))
    moved = shifted(reach, 4)
    v4 = window(24, 8, pattern, v4)
    moved, v4 = lax.optimization_barrier((moved, v4))
    v4_far = shifted(v4, 4)
    v4_other = swap(v4)
    reach = reach + apply(moved, 4, v4, v4_other)
    moved = shifted(reach, 8)
    gain_own, reach = lax.optimization_barrier((smoother_gain.T, reach))
    gain_own = call(gain_kernel, shape(panel, width), [SMEM, VMEM], (places, gain_own), "gain", 8)
    gain_mine = along(gain_own)
    v4_far, moved, *gain_mine = lax.optimization_barrier((v4_far, moved, *gain_mine))
    v4_far_other = swap(v4_far)
    gain_theirs = [swap(a) for a in gain_mine]
    v8, v8_other = call(
        join_kernel,
        (shape(width, half),) * 2,
        [SMEM, SMEM] + [VMEM] * 4,
        (cores, (block >= 4).reshape(1).astype(jnp.int32), v4_far, v4_far_other, v4, v4_other),
        "join",
        1.5,
    )
    mean = reach + apply(moved, 8, v8, v8_other)
    gain_mine[0], mean = lax.optimization_barrier((gain_mine[0], mean))
    gain = [*gain_mine, *gain_theirs]
    moved = shifted(mean, 8)
    gh, gl, g4h, g4l, kh, kl, g4 = call(
        powers_kernel,
        (bf(), bf(), bf(), bf(), bf(), bf(), shape(width, width)),
        [SMEM] + [VMEM] * 10,
        (places, *gain, bh, bl),
        "powers",
        12,
    )
    moved, g4 = lax.optimization_barrier((moved, g4))
    mean = reach + apply(moved, 8, v8, v8_other)
    mean, g4 = lax.optimization_barrier((mean, g4))
    moved = shifted(mean, 8)
    p1, p2 = call(middle_kernel, (shape(width, width),) * 2, [VMEM], (g4,), "middle", 12)
    p4, p8, p16 = call(far_kernel, (shape(width, width),) * 3, [VMEM], (p2,), "far", 12)
    moved, p4 = lax.optimization_barrier((moved, p4))
    mean = reach + apply(moved, 8, v8, v8_other)
    mean = jnp.where(block == 0, initial_mean, mean)

    far = (p1, p2, p4, p8, p16)

    final = block == count - 1
    filtered, gap, part, back, virtual = call(
        forward_kernel,
        (
            shape(steps, trials, width),
            shape(4, steps // 4, trials, width),
            shape(4, trials, width),
            shape(trials, width),
            shape(trials, width),
        ),
        [SMEM, SMEM] + [VMEM] * 12,
        (mask, final.reshape(1).astype(jnp.int32), mean, drive, inputs, pair, bh, bl, gh, gl, g4h, g4l, kh, kl),
        "forward",
        10,
    )

    scan = lax.all_to_all(back, "tm", 0, 0, tiled=True)
    for k in range(5):
        ahead = jnp.concatenate([scan[2**k :], jnp.zeros((2**k, width), F32)], 0)
        scan = scan + ahead + high_dot(ahead, far[k])
    ahead = jnp.concatenate([scan[1:], jnp.zeros((1, width), F32)], 0)
    back_in = lax.all_to_all(ahead, "tm", 0, 0, tiled=True)
    smoothed = call(
        backward_kernel,
        shape(4, steps // 4, trials, width),
        [VMEM] * 7,
        (jnp.where(final, virtual, back_in), gap, part, gh, gl, g4h, g4l),
        "backward",
        3,
    )
    return filtered, smoothed.reshape(steps, trials, width)


def solution(mesh):
    placed = (
        P("tm", "state", None),
        P("tm"),
        P(None, "state"),
        P(None, "state"),
        P(None, "state"),
        P(),
        P("state", None),
    )
    return jax.shard_map(
        local,
        mesh=mesh,
        in_specs=placed,
        out_specs=(P("tm", "state", None), P("tm", "state", None)),
        check_vma=False,
    )
```

```python
import functools

import jax
import jax.numpy as jnp
from jax import lax
from jax.experimental import pallas as pl
from jax.experimental.pallas import tpu as pltpu
from jax.sharding import PartitionSpec as P

F32 = jnp.float32
BF16 = jnp.bfloat16
VMEM = pl.BlockSpec(memory_space=pltpu.VMEM)
SMEM = pl.BlockSpec(memory_space=pltpu.SMEM)
LIMIT = 16 * 1024 * 1024


def split(a):
    high = a.astype(BF16)
    return high, (a - high.astype(F32)).astype(BF16)


def dot(left, right):
    return jnp.dot(left, right, preferred_element_type=F32)


def dot3(a, high, low):
    rows = a.shape[0]
    a_high, a_low = split(a)
    both = dot(jnp.concatenate([a_high, a_low], 0), high)
    return both[:rows] + both[rows:] + dot(a_high, low)


def call(kernel, outs, specs, args, name, micros, scratch=(), out_specs=None):
    return pl.pallas_call(
        kernel,
        out_shape=outs,
        in_specs=specs,
        out_specs=jax.tree.map(lambda _: VMEM, outs) if out_specs is None else out_specs,
        scratch_shapes=list(scratch),
        compiler_params=pltpu.CompilerParams(vmem_limit_bytes=LIMIT),
        cost_estimate=pl.CostEstimate(flops=int(micros * 1.15e9), bytes_accessed=1 << 20, transcendentals=0),
        name=name,
    )(*args)


def shape(*dims, dtype=F32):
    return jax.ShapeDtypeStruct(dims, dtype)


def drive_kernel(mask_ref, frames_ref, gain_ref, out_ref, flags_ref):
    high, low = split(gain_ref[...])
    frames = frames_ref[...]
    turned = (((1,), (1,)), ((), ()))
    drive = lax.dot_general(frames, high, turned, preferred_element_type=F32)
    drive = drive + lax.dot_general(frames, low, turned, preferred_element_type=F32)
    steps, trials, _ = out_ref.shape
    for t in range(steps):
        out_ref[t] = drive[t * trials : (t + 1) * trials] * mask_ref[t].astype(F32)
        flags_ref[t] = mask_ref[t]


PIECES = ((0, 0), (1, 0), (2, 0), (3, 0))


def gathered(place_ref, pieces, write):
    width = pieces[0].shape[-1]
    size = pieces[0].shape[-2]
    chips = width // (2 * size)
    place = place_ref[0]
    for i, piece in enumerate(pieces):
        away, first = PIECES[i % len(PIECES)]
        panel = piece.shape[-2]
        core = lax.rem(place + (0 if i < len(PIECES) else 1), 2)
        source = 2 * lax.rem(lax.div(place, 2) + chips - away, chips) + core
        row = pl.multiple_of(source * size + first, panel)
        across = lax.broadcasted_iota(jnp.int32, (panel, width), 1)
        down = lax.broadcasted_iota(jnp.int32, (panel, width), 0) + row
        write(pl.ds(row, panel), piece, jnp.where(across == down, 1.0, 0.0).astype(F32))


def gain_kernel(place_ref, own_ref, out_ref):
    panel, width = own_ref.shape
    across = lax.broadcasted_iota(jnp.int32, (panel, width), 1)
    down = lax.broadcasted_iota(jnp.int32, (panel, width), 0) + place_ref[0] * panel
    out_ref[...] = own_ref[...] - jnp.where(across == down, 1.0, 0.0).astype(F32)


def compose(eh, el, lh, ll):
    product = dot(eh, lh) + dot(el, lh) + dot(eh, ll)
    whole = eh.astype(F32) + el.astype(F32) + lh.astype(F32) + ll.astype(F32)
    return split(product + whole)


def chosen_step(rows, flags, high_ref, low_ref):
    parts = [dot3(rows, high_ref[m], low_ref[m]) for m in range(2)]
    size = rows.shape[0] // len(flags)
    return [
        jnp.where(flag > 0, parts[1][i * size : (i + 1) * size], parts[0][i * size : (i + 1) * size])
        for i, flag in enumerate(flags)
    ]


def local_kernel(place_ref, mask_ref, *refs):
    pieces, (drive_ref, start_ref, last_ref, input_ref, high_ref, low_ref, pair_ref) = refs[:8], refs[8:]
    pairs, trials, width = input_ref.shape

    def write(rows, piece, eye):
        for m in range(2):
            high, low = split(piece[m] - eye)
            high_ref[m, rows, :] = high
            low_ref[m, rows, :] = low

    gathered(place_ref, pieces, write)

    def pair(i, _):
        first, second = lax.rem(i, 2), lax.div(i, 2)
        pair_ref[i, 0], pair_ref[i, 1] = compose(high_ref[first], low_ref[first], high_ref[second], low_ref[second])
        return 0

    lax.fori_loop(0, 4, pair, 0)
    for start in range(0, pairs, 4):
        some = range(start, start + 4)
        rows = jnp.concatenate([drive_ref[2 * i] for i in some], 0)
        moved = chosen_step(rows, [mask_ref[2 * i + 1] for i in some], high_ref, low_ref)
        for i, part in zip(some, moved):
            input_ref[i] = drive_ref[2 * i] + part + drive_ref[2 * i + 1]

    def step(i, mean):
        p = mask_ref[2 * i] + 2 * mask_ref[2 * i + 1]
        return mean + dot3(mean, pair_ref[p, 0], pair_ref[p, 1]) + input_ref[i]

    last_ref[...] = lax.fori_loop(0, pairs, step, start_ref[...])


def window_kernel(begin, count, core_ref, pattern_ref, pair_ref, *refs):
    out_ref = refs[-1]
    width, half = out_ref.shape
    if begin == 0:
        across = lax.broadcasted_iota(jnp.int32, (width, half), 1) + core_ref[0] * half
        down = lax.broadcasted_iota(jnp.int32, (width, half), 0)
        out_ref[...] = jnp.where(across == down, 1.0, 0.0).astype(F32)
    else:
        out_ref[...] = refs[0][...]
    extend(begin, count, pattern_ref, pair_ref, out_ref)


def extend(begin, count, pattern_ref, pair_ref, out_ref):
    end = pattern_ref.shape[0] - 2 - 2 * begin

    def step(i, _):
        p = pattern_ref[end - 2 * i] + 2 * pattern_ref[end - 2 * i + 1]

        @pl.when(p < 4)
        def _():
            high, low = split(out_ref[...])
            out_ref[...] += dot(pair_ref[p, 0], high) + dot(pair_ref[p, 1], high) + dot(pair_ref[p, 0], low)

        return 0

    lax.fori_loop(0, count, step, 0)


def join_kernel(begin, count, core_ref, pattern_ref, pair_ref, valid_ref, far_ref, far_other_ref, near_ref, out_ref):
    half = near_ref.shape[1]
    total = jnp.zeros(out_ref.shape, F32)
    for side, part_ref in ((core_ref[0], far_ref), (1 - core_ref[0], far_other_ref)):
        rows = pl.ds(pl.multiple_of(side * half, half), half)
        part = part_ref[...]
        part_high, part_low = split(jnp.where(valid_ref[0] > 0, part, jnp.zeros_like(part)))
        high, low = split(near_ref[rows, :])
        total = total + dot(part_high, high) + dot(part_low, high) + dot(part_high, low)
    out_ref[...] = total
    extend(begin, count, pattern_ref, pair_ref, out_ref)


def square(ref):
    high, low = split(ref[...])
    ref[...] = 2.0 * ref[...] + dot(high, high) + dot(low, high) + dot(high, low)


def powers_kernel(place_ref, *refs):
    pieces = refs[:8]
    fh_ref, fl_ref, gh_ref, gl_ref, g4h_ref, g4l_ref, kh_ref, kl_ref, now_ref = refs[8:]

    def write(rows, piece, _):
        now_ref[rows, :] = piece[...]

    gathered(place_ref, pieces, write)
    high, low = split(now_ref[...])
    gh_ref[...], gl_ref[...] = high, low
    product = dot(fh_ref[0], high) + dot(fl_ref[0], high) + dot(fh_ref[0], low)
    both = fh_ref[0].astype(F32) + fl_ref[0].astype(F32) + now_ref[...]
    kh_ref[...], kl_ref[...] = split(product + both)
    square(now_ref)
    square(now_ref)
    g4h_ref[...], g4l_ref[...] = split(now_ref[...])


def middle_kernel(now_ref, p1_ref, p2_ref):
    p1_ref[...] = now_ref[...]
    square(p1_ref)
    square(p1_ref)
    p2_ref[...] = p1_ref[...]
    square(p2_ref)


def far_kernel(p2_ref, p4_ref, p8_ref, p16_ref):
    p4_ref[...] = p2_ref[...]
    square(p4_ref)
    p8_ref[...] = p4_ref[...]
    square(p8_ref)
    p16_ref[...] = p8_ref[...]
    square(p16_ref)


def forward_kernel(mask_ref, final_ref, start_ref, drive_ref, input_ref, pair_ref, bh_ref, bl_ref, gh_ref, gl_ref,
                   g4h_ref, g4l_ref, kh_ref, kl_ref, filtered_ref, gap_ref, part_ref, back_ref, virtual_ref):
    steps, trials, width = drive_ref.shape
    groups, inner = gap_ref.shape[:2]

    def step(i, mean):
        p = mask_ref[2 * i] + 2 * mask_ref[2 * i + 1]
        mean = mean + dot3(mean, pair_ref[p, 0], pair_ref[p, 1]) + input_ref[i]
        filtered_ref[2 * i + 1] = mean
        return mean

    last = lax.fori_loop(0, steps // 2, step, start_ref[...])
    for start in range(0, steps, 8):
        some = range(start, start + 8, 2)
        rows = [start_ref[...] if t == 0 else filtered_ref[t - 1] for t in some]
        moved = chosen_step(jnp.concatenate(rows, 0), [mask_ref[t] for t in some], bh_ref, bl_ref)
        for t, row, part in zip(some, rows, moved):
            filtered_ref[t] = row + part + drive_ref[t]
    virtual = last + dot3(last, bh_ref[0], bl_ref[0])
    virtual_ref[...] = virtual
    for g in range(groups):
        flat = filtered_ref[g * inner : (g + 1) * inner].reshape(inner * trials, width)
        gap_ref[g] = -dot3(flat, kh_ref[...], kl_ref[...]).reshape(inner, trials, width)
    value = gap_ref[:, inner - 1].reshape(groups * trials, width)
    for j in range(inner - 2, -1, -1):
        value = value + dot3(value, gh_ref[...], gl_ref[...]) + gap_ref[:, j].reshape(groups * trials, width)
    part = value.reshape(groups, trials, width)
    part_ref[...] = part
    carry = jnp.where(final_ref[0] > 0, virtual, jnp.zeros_like(virtual))
    for g in range(groups - 1, -1, -1):
        carry = carry + dot3(carry, g4h_ref[...], g4l_ref[...]) + part[g]
    back_ref[...] = carry


def backward_kernel(start_ref, gap_ref, part_ref, gh_ref, gl_ref, g4h_ref, g4l_ref, out_ref):
    groups, inner, trials, width = gap_ref.shape
    carry = start_ref[...]
    starts = [carry]
    for g in range(groups - 1, 0, -1):
        carry = carry + dot3(carry, g4h_ref[...], g4l_ref[...]) + part_ref[g]
        starts.insert(0, carry)
    value = jnp.concatenate(starts, 0)
    for j in range(inner - 1, -1, -1):
        value = value + dot3(value, gh_ref[...], gl_ref[...]) + gap_ref[:, j].reshape(groups * trials, width)
        out_ref[:, j] = value.reshape(groups, trials, width)


def high_dot(left, right):
    return jnp.dot(left, right, precision=lax.Precision.HIGH, preferred_element_type=F32)


def local(observations, mask, transition, updated_transition, smoother_gain, obs_gain, initial_mean):
    steps, trials, channels = observations.shape
    width, panel = transition.shape
    count = lax.axis_size("tm")
    chips = lax.axis_size("state") // 2
    block = lax.axis_index("tm")
    place = lax.axis_index("state")
    chip, core = place // 2, place % 2

    def along_x(a, k):
        return lax.ppermute(
            a, "state", [(2 * i + c, 2 * ((i + k) % chips) + c) for i in range(chips) for c in range(2)]
        )

    def swap(a):
        return lax.ppermute(a, "state", [(2 * i + c, 2 * i + 1 - c) for i in range(chips) for c in range(2)])

    def shifted(a, k):
        return lax.ppermute(a, "tm", [(i, (i + k) % count) for i in range(count)])

    def along(own):
        return [own] + [along_x(own, k) for k in (1, 2, 3)]

    own = jnp.stack([transition.T, updated_transition.T])
    mine = along(own)
    own, mine[3] = lax.optimization_barrier((own, mine[3]))
    theirs = [swap(a) for a in (own, *mine[1:])]
    places = place.reshape(1).astype(jnp.int32)

    drive, flags = call(
        drive_kernel,
        (shape(steps, trials, width), shape(steps, dtype=jnp.int32)),
        [SMEM, VMEM, VMEM],
        (mask, observations.reshape(steps * trials, channels), obs_gain),
        "drive",
        2,
        out_specs=(VMEM, SMEM),
    )
    recent = jnp.concatenate([jnp.where(block >= k, shifted(flags, k), 2) for k in (2, 1)])
    pattern = jnp.concatenate([jnp.where(block >= 2, shifted(recent, 2), 2), recent])
    longer = jnp.concatenate([jnp.where(block >= 4, shifted(pattern, 4), 2), pattern])

    start = jnp.where(block == 0, initial_mean, jnp.zeros_like(initial_mean))
    bf = functools.partial(shape, width, width, dtype=BF16)
    two = shape(2, width, width, dtype=BF16)
    last, inputs, bh, bl, pair = call(
        local_kernel,
        (shape(trials, width), shape(steps // 2, trials, width), two, two, shape(4, 2, width, width, dtype=BF16)),
        [SMEM, SMEM] + [VMEM] * 10,
        (places, mask, *mine, *theirs, drive, start),
        "local",
        9,
    )

    half = width // 2
    cores = core.reshape(1).astype(jnp.int32)

    def window(begin, count, pattern, *first, claim=5):
        return call(
            functools.partial(window_kernel, begin, count),
            shape(width, half),
            [SMEM, SMEM, VMEM] + [VMEM] * len(first),
            (cores, pattern, pair, *first),
            f"window{begin + count}",
            claim,
        )

    def apply(mean, k, mine, theirs):
        mean = jnp.where(block >= k, mean, 0.0)
        here, there = high_dot(mean, mine), high_dot(mean, theirs)
        return jnp.where(
            core == 0, jnp.concatenate([here, there], 1), jnp.concatenate([there, here], 1)
        )

    one, two_back = shifted(last, 1), shifted(last, 2)
    v1 = window(0, 8, recent)
    v1_other = swap(v1)
    v2 = window(8, 8, pattern, v1)
    v1, v1_other, v2 = lax.optimization_barrier((v1, v1_other, v2))
    reach = jnp.where(block >= 1, one, 0.0) + apply(two_back, 2, v1, v1_other)

    reach, v2 = lax.optimization_barrier((reach, v2))
    moved = shifted(reach, 2)
    v2_other = swap(v2)
    v2_far = shifted(v2, 4)
    v4 = window(16, 8, pattern, v2, claim=0.5)
    v2, v2_other, v4 = lax.optimization_barrier((v2, v2_other, v4))
    reach = reach + apply(moved, 2, v2, v2_other)

    reach, v4 = lax.optimization_barrier((reach, v4))
    moved = shifted(reach, 4)
    v2_far_other = swap(v2_far)
    v4 = window(24, 8, pattern, v4, claim=5)
    moved, v4 = lax.optimization_barrier((moved, v4))
    v4_other = swap(v4)
    reach = reach + apply(moved, 4, v4, v4_other)
    moved = shifted(reach, 8)
    v8 = call(
        functools.partial(join_kernel, 48, 16),
        shape(width, half),
        [SMEM, SMEM, VMEM, SMEM] + [VMEM] * 3,
        (cores, longer, pair, (block >= 4).reshape(1).astype(jnp.int32), v2_far, v2_far_other, v4),
        "join",
        11,
    )
    moved, v8 = lax.optimization_barrier((moved, v8))
    v8_other = swap(v8)
    mean = reach + apply(moved, 8, v8, v8_other)
    gain_own, mean = lax.optimization_barrier((smoother_gain.T, mean))
    moved = shifted(mean, 8)
    gain_own = call(gain_kernel, shape(panel, width), [SMEM, VMEM], (places, gain_own), "gain", 8)
    gain_mine = along(gain_own)
    moved, *gain_mine = lax.optimization_barrier((moved, *gain_mine))
    gain_theirs = [swap(a) for a in gain_mine]
    gain = [*gain_mine, *gain_theirs]
    mean = reach + apply(moved, 8, v8, v8_other)
    gain[0], mean = lax.optimization_barrier((gain[0], mean))
    moved = shifted(mean, 8)
    gh, gl, g4h, g4l, kh, kl, g4 = call(
        powers_kernel,
        (bf(), bf(), bf(), bf(), bf(), bf(), shape(width, width)),
        [SMEM] + [VMEM] * 10,
        (places, *gain, bh, bl),
        "powers",
        12,
    )
    moved, g4 = lax.optimization_barrier((moved, g4))
    mean = reach + apply(moved, 8, v8, v8_other)
    p1, p2 = call(middle_kernel, (shape(width, width),) * 2, [VMEM], (g4,), "middle", 4)
    p4, p8, p16 = call(far_kernel, (shape(width, width),) * 3, [VMEM], (p2,), "far", 4)
    mean = jnp.where(block == 0, initial_mean, mean)

    far = (p1, p2, p4, p8, p16)

    final = block == count - 1
    filtered, gap, part, back, virtual = call(
        forward_kernel,
        (
            shape(steps, trials, width),
            shape(4, steps // 4, trials, width),
            shape(4, trials, width),
            shape(trials, width),
            shape(trials, width),
        ),
        [SMEM, SMEM] + [VMEM] * 12,
        (mask, final.reshape(1).astype(jnp.int32), mean, drive, inputs, pair, bh, bl, gh, gl, g4h, g4l, kh, kl),
        "forward",
        10,
    )

    scan = lax.all_to_all(back, "tm", 0, 0, tiled=True)
    for k in range(5):
        ahead = jnp.concatenate([scan[2**k :], jnp.zeros((2**k, width), F32)], 0)
        scan = scan + ahead + high_dot(ahead, far[k])
    ahead = jnp.concatenate([scan[1:], jnp.zeros((1, width), F32)], 0)
    back_in = lax.all_to_all(ahead, "tm", 0, 0, tiled=True)
    smoothed = call(
        backward_kernel,
        shape(4, steps // 4, trials, width),
        [VMEM] * 7,
        (jnp.where(final, virtual, back_in), gap, part, gh, gl, g4h, g4l),
        "backward",
        3,
    )
    return filtered, smoothed.reshape(steps, trials, width)


def solution(mesh):
    placed = (
        P("tm", "state", None),
        P("tm"),
        P(None, "state"),
        P(None, "state"),
        P(None, "state"),
        P(),
        P("state", None),
    )
    return jax.shard_map(
        local,
        mesh=mesh,
        in_specs=placed,
        out_specs=(P("tm", "state", None), P("tm", "state", None)),
        check_vma=False,
    )
```

```python
import functools

import jax
import jax.numpy as jnp
from jax import lax
from jax.experimental import pallas as pl
from jax.experimental.pallas import tpu as pltpu
from jax.sharding import PartitionSpec as P

F32 = jnp.float32
BF16 = jnp.bfloat16
VMEM = pl.BlockSpec(memory_space=pltpu.VMEM)
SMEM = pl.BlockSpec(memory_space=pltpu.SMEM)
LIMIT = 16 * 1024 * 1024


def split(a):
    high = a.astype(BF16)
    return high, (a - high.astype(F32)).astype(BF16)


def dot(left, right):
    return jnp.dot(left, right, preferred_element_type=F32)


def dot3(a, high, low):
    rows = a.shape[0]
    a_high, a_low = split(a)
    both = dot(jnp.concatenate([a_high, a_low], 0), high)
    return both[:rows] + both[rows:] + dot(a_high, low)


def call(kernel, outs, specs, args, name, micros, scratch=(), out_specs=None):
    return pl.pallas_call(
        kernel,
        out_shape=outs,
        in_specs=specs,
        out_specs=jax.tree.map(lambda _: VMEM, outs) if out_specs is None else out_specs,
        scratch_shapes=list(scratch),
        compiler_params=pltpu.CompilerParams(vmem_limit_bytes=LIMIT),
        cost_estimate=pl.CostEstimate(flops=int(micros * 1.15e9), bytes_accessed=1 << 20, transcendentals=0),
        name=name,
    )(*args)


def shape(*dims, dtype=F32):
    return jax.ShapeDtypeStruct(dims, dtype)


def drive_kernel(mask_ref, frames_ref, gain_ref, out_ref, flags_ref):
    high, low = split(gain_ref[...])
    frames = frames_ref[...]
    turned = (((1,), (1,)), ((), ()))
    drive = lax.dot_general(frames, high, turned, preferred_element_type=F32)
    drive = drive + lax.dot_general(frames, low, turned, preferred_element_type=F32)
    steps, trials, _ = out_ref.shape
    for t in range(steps):
        out_ref[t] = drive[t * trials : (t + 1) * trials] * mask_ref[t].astype(F32)
        flags_ref[t] = mask_ref[t]


PIECES = ((0, 0), (1, 0), (2, 0), (3, 0))


def gathered(place_ref, pieces, write):
    width = pieces[0].shape[-1]
    size = pieces[0].shape[-2]
    chips = width // (2 * size)
    place = place_ref[0]
    for i, piece in enumerate(pieces):
        away, first = PIECES[i % len(PIECES)]
        panel = piece.shape[-2]
        core = lax.rem(place + (0 if i < len(PIECES) else 1), 2)
        source = 2 * lax.rem(lax.div(place, 2) + chips - away, chips) + core
        row = pl.multiple_of(source * size + first, panel)
        across = lax.broadcasted_iota(jnp.int32, (panel, width), 1)
        down = lax.broadcasted_iota(jnp.int32, (panel, width), 0) + row
        write(pl.ds(row, panel), piece, jnp.where(across == down, 1.0, 0.0).astype(F32))


def gain_kernel(place_ref, own_ref, out_ref):
    panel, width = own_ref.shape
    across = lax.broadcasted_iota(jnp.int32, (panel, width), 1)
    down = lax.broadcasted_iota(jnp.int32, (panel, width), 0) + place_ref[0] * panel
    out_ref[...] = own_ref[...] - jnp.where(across == down, 1.0, 0.0).astype(F32)


def compose(eh, el, lh, ll):
    product = dot(eh, lh) + dot(el, lh) + dot(eh, ll)
    whole = eh.astype(F32) + el.astype(F32) + lh.astype(F32) + ll.astype(F32)
    return split(product + whole)


def chosen_step(rows, flags, high_ref, low_ref):
    parts = [dot3(rows, high_ref[m], low_ref[m]) for m in range(2)]
    size = rows.shape[0] // len(flags)
    return [
        jnp.where(flag > 0, parts[1][i * size : (i + 1) * size], parts[0][i * size : (i + 1) * size])
        for i, flag in enumerate(flags)
    ]


def local_kernel(place_ref, mask_ref, *refs):
    pieces, (drive_ref, start_ref, last_ref, input_ref, high_ref, low_ref, pair_ref) = refs[:8], refs[8:]
    pairs, trials, width = input_ref.shape

    def write(rows, piece, eye):
        for m in range(2):
            high, low = split(piece[m] - eye)
            high_ref[m, rows, :] = high
            low_ref[m, rows, :] = low

    gathered(place_ref, pieces, write)

    for i in range(4):
        first, second = i % 2, i // 2
        pair_ref[i, 0], pair_ref[i, 1] = compose(high_ref[first], low_ref[first], high_ref[second], low_ref[second])
    for start in range(0, pairs, 8):
        some = range(start, start + 8)
        rows = jnp.concatenate([drive_ref[2 * i] for i in some], 0)
        moved = chosen_step(rows, [mask_ref[2 * i + 1] for i in some], high_ref, low_ref)
        for i, part in zip(some, moved):
            input_ref[i] = drive_ref[2 * i] + part + drive_ref[2 * i + 1]

    def step(i, mean):
        p = mask_ref[2 * i] + 2 * mask_ref[2 * i + 1]
        return mean + dot3(mean, pair_ref[p, 0], pair_ref[p, 1]) + input_ref[i]

    last_ref[...] = lax.fori_loop(0, pairs, step, start_ref[...], unroll=True)


def window_kernel(begin, count, core_ref, pattern_ref, pair_ref, *refs):
    out_ref = refs[-1]
    width, half = out_ref.shape
    if begin == 0:
        across = lax.broadcasted_iota(jnp.int32, (width, half), 1) + core_ref[0] * half
        down = lax.broadcasted_iota(jnp.int32, (width, half), 0)
        out_ref[...] = jnp.where(across == down, 1.0, 0.0).astype(F32)
    else:
        out_ref[...] = refs[0][...]
    end = pattern_ref.shape[0] - 2 - 2 * begin

    def step(i, _):
        p = pattern_ref[end - 2 * i] + 2 * pattern_ref[end - 2 * i + 1]

        @pl.when(p < 4)
        def _():
            high, low = split(out_ref[...])
            out_ref[...] += dot(pair_ref[p, 0], high) + dot(pair_ref[p, 1], high) + dot(pair_ref[p, 0], low)

        return 0

    lax.fori_loop(0, count, step, 0, unroll=2)


def join_kernel(core_ref, valid_ref, far_ref, far_other_ref, near_ref, near_other_ref, out_ref, out_other_ref):
    half = near_ref.shape[1]
    total, total_other = jnp.zeros(out_ref.shape, F32), jnp.zeros(out_ref.shape, F32)
    for side, part_ref in ((core_ref[0], far_ref), (1 - core_ref[0], far_other_ref)):
        rows = pl.ds(pl.multiple_of(side * half, half), half)
        part = part_ref[...]
        part_high, part_low = split(jnp.where(valid_ref[0] > 0, part, jnp.zeros_like(part)))

        def times(ref):
            high, low = split(ref[rows, :])
            return dot(part_high, high) + dot(part_low, high) + dot(part_high, low)

        total, total_other = total + times(near_ref), total_other + times(near_other_ref)
    out_ref[...], out_other_ref[...] = total, total_other


def square(ref):
    high, low = split(ref[...])
    ref[...] = 2.0 * ref[...] + dot(high, high) + dot(low, high) + dot(high, low)


def powers_kernel(place_ref, *refs):
    pieces = refs[:8]
    fh_ref, fl_ref, gh_ref, gl_ref, g4h_ref, g4l_ref, kh_ref, kl_ref, now_ref = refs[8:]

    def write(rows, piece, _):
        now_ref[rows, :] = piece[...]

    gathered(place_ref, pieces, write)
    high, low = split(now_ref[...])
    gh_ref[...], gl_ref[...] = high, low
    product = dot(fh_ref[0], high) + dot(fl_ref[0], high) + dot(fh_ref[0], low)
    both = fh_ref[0].astype(F32) + fl_ref[0].astype(F32) + now_ref[...]
    kh_ref[...], kl_ref[...] = split(product + both)
    square(now_ref)
    square(now_ref)
    g4h_ref[...], g4l_ref[...] = split(now_ref[...])


def middle_kernel(now_ref, p1_ref, p2_ref):
    p1_ref[...] = now_ref[...]
    square(p1_ref)
    square(p1_ref)
    p2_ref[...] = p1_ref[...]
    square(p2_ref)


def far_kernel(p2_ref, p4_ref, p8_ref, p16_ref):
    p4_ref[...] = p2_ref[...]
    square(p4_ref)
    p8_ref[...] = p4_ref[...]
    square(p8_ref)
    p16_ref[...] = p8_ref[...]
    square(p16_ref)


def forward_kernel(mask_ref, final_ref, start_ref, drive_ref, input_ref, pair_ref, bh_ref, bl_ref, gh_ref, gl_ref,
                   g4h_ref, g4l_ref, kh_ref, kl_ref, filtered_ref, gap_ref, part_ref, back_ref, virtual_ref):
    steps, trials, width = drive_ref.shape
    groups, inner = gap_ref.shape[:2]

    def step(i, mean):
        p = mask_ref[2 * i] + 2 * mask_ref[2 * i + 1]
        mean = mean + dot3(mean, pair_ref[p, 0], pair_ref[p, 1]) + input_ref[i]
        filtered_ref[2 * i + 1] = mean
        return mean

    last = lax.fori_loop(0, steps // 2, step, start_ref[...], unroll=True)
    for start in range(0, steps, 16):
        some = range(start, start + 16, 2)
        rows = [start_ref[...] if t == 0 else filtered_ref[t - 1] for t in some]
        moved = chosen_step(jnp.concatenate(rows, 0), [mask_ref[t] for t in some], bh_ref, bl_ref)
        for t, row, part in zip(some, rows, moved):
            filtered_ref[t] = row + part + drive_ref[t]
    virtual = last + dot3(last, bh_ref[0], bl_ref[0])
    virtual_ref[...] = virtual
    flat = filtered_ref[...].reshape(steps * trials, width)
    gap_ref[...] = -dot3(flat, kh_ref[...], kl_ref[...]).reshape(groups, inner, trials, width)
    value = gap_ref[:, inner - 1].reshape(groups * trials, width)
    for j in range(inner - 2, -1, -1):
        value = value + dot3(value, gh_ref[...], gl_ref[...]) + gap_ref[:, j].reshape(groups * trials, width)
    part = value.reshape(groups, trials, width)
    part_ref[...] = part
    carry = jnp.where(final_ref[0] > 0, virtual, jnp.zeros_like(virtual))
    for g in range(groups - 1, -1, -1):
        carry = carry + dot3(carry, g4h_ref[...], g4l_ref[...]) + part[g]
    back_ref[...] = carry


def backward_kernel(start_ref, gap_ref, part_ref, gh_ref, gl_ref, g4h_ref, g4l_ref, out_ref):
    groups, inner, trials, width = gap_ref.shape
    carry = start_ref[...]
    starts = [carry]
    for g in range(groups - 1, 0, -1):
        carry = carry + dot3(carry, g4h_ref[...], g4l_ref[...]) + part_ref[g]
        starts.insert(0, carry)
    value = jnp.concatenate(starts, 0)
    for j in range(inner - 1, -1, -1):
        value = value + dot3(value, gh_ref[...], gl_ref[...]) + gap_ref[:, j].reshape(groups * trials, width)
        out_ref[:, j] = value.reshape(groups, trials, width)


def high_dot(left, right):
    return jnp.dot(left, right, precision=lax.Precision.HIGH, preferred_element_type=F32)


def local(observations, mask, transition, updated_transition, smoother_gain, obs_gain, initial_mean):
    steps, trials, channels = observations.shape
    width, panel = transition.shape
    count = lax.axis_size("tm")
    chips = lax.axis_size("state") // 2
    block = lax.axis_index("tm")
    place = lax.axis_index("state")
    chip, core = place // 2, place % 2

    def along_x(a, k):
        return lax.ppermute(
            a, "state", [(2 * i + c, 2 * ((i + k) % chips) + c) for i in range(chips) for c in range(2)]
        )

    def swap(a):
        return lax.ppermute(a, "state", [(2 * i + c, 2 * i + 1 - c) for i in range(chips) for c in range(2)])

    def shifted(a, k):
        return lax.ppermute(a, "tm", [(i, (i + k) % count) for i in range(count)])

    def along(own):
        return [own] + [along_x(own, k) for k in (1, 2, 3)]

    own = jnp.stack([transition.T, updated_transition.T])
    mine = along(own)
    own, mine[3] = lax.optimization_barrier((own, mine[3]))
    theirs = [swap(a) for a in (own, *mine[1:])]
    places = place.reshape(1).astype(jnp.int32)

    drive, flags = call(
        drive_kernel,
        (shape(steps, trials, width), shape(steps, dtype=jnp.int32)),
        [SMEM, VMEM, VMEM],
        (mask, observations.reshape(steps * trials, channels), obs_gain),
        "drive",
        2,
        out_specs=(VMEM, SMEM),
    )
    recent = jnp.concatenate([jnp.where(block >= k, shifted(flags, k), 2) for k in (2, 1)])
    pattern = jnp.concatenate([jnp.where(block >= 2, shifted(recent, 2), 2), recent])

    start = jnp.where(block == 0, initial_mean, jnp.zeros_like(initial_mean))
    bf = functools.partial(shape, width, width, dtype=BF16)
    two = shape(2, width, width, dtype=BF16)
    last, inputs, bh, bl, pair = call(
        local_kernel,
        (shape(trials, width), shape(steps // 2, trials, width), two, two, shape(4, 2, width, width, dtype=BF16)),
        [SMEM, SMEM] + [VMEM] * 10,
        (places, mask, *mine, *theirs, drive, start),
        "local",
        9,
    )

    half = width // 2
    cores = core.reshape(1).astype(jnp.int32)

    def window(begin, count, pattern, *first):
        return call(
            functools.partial(window_kernel, begin, count),
            shape(width, half),
            [SMEM, SMEM, VMEM] + [VMEM] * len(first),
            (cores, pattern, pair, *first),
            f"window{begin + count}",
            0.6 * count,
        )

    def apply(mean, k, mine, theirs):
        mean = jnp.where(block >= k, mean, 0.0)
        here, there = high_dot(mean, mine), high_dot(mean, theirs)
        return jnp.where(
            core == 0, jnp.concatenate([here, there], 1), jnp.concatenate([there, here], 1)
        )

    one, two_back = shifted(last, 1), shifted(last, 2)
    v1 = window(0, 8, recent)
    v1_other = swap(v1)
    v2 = window(8, 8, recent, v1)
    v1, v1_other, v2 = lax.optimization_barrier((v1, v1_other, v2))
    reach = jnp.where(block >= 1, one, 0.0) + apply(two_back, 2, v1, v1_other)

    reach, v2 = lax.optimization_barrier((reach, v2))
    moved = shifted(reach, 2)
    v2_other = swap(v2)
    v4 = window(16, 8, pattern, v2)
    v2, v2_other, v4 = lax.optimization_barrier((v2, v2_other, v4))
    reach = reach + apply(moved, 2, v2, v2_other)

    reach, v4 = lax.optimization_barrier((reach, v4))
    moved = shifted(reach, 4)
    v4 = window(24, 8, pattern, v4)
    moved, v4 = lax.optimization_barrier((moved, v4))
    v4_far = shifted(v4, 4)
    v4_other = swap(v4)
    reach = reach + apply(moved, 4, v4, v4_other)
    moved = shifted(reach, 8)
    gain_own, reach = lax.optimization_barrier((smoother_gain.T, reach))
    gain_own = call(gain_kernel, shape(panel, width), [SMEM, VMEM], (places, gain_own), "gain", 8)
    gain_mine = along(gain_own)
    v4_far, moved, *gain_mine = lax.optimization_barrier((v4_far, moved, *gain_mine))
    v4_far_other = swap(v4_far)
    gain_theirs = [swap(a) for a in gain_mine]
    v8, v8_other = call(
        join_kernel,
        (shape(width, half),) * 2,
        [SMEM, SMEM] + [VMEM] * 4,
        (cores, (block >= 4).reshape(1).astype(jnp.int32), v4_far, v4_far_other, v4, v4_other),
        "join",
        1.5,
    )
    mean = reach + apply(moved, 8, v8, v8_other)
    gain_mine[0], mean = lax.optimization_barrier((gain_mine[0], mean))
    gain = [*gain_mine, *gain_theirs]
    moved = shifted(mean, 8)
    gh, gl, g4h, g4l, kh, kl, g4 = call(
        powers_kernel,
        (bf(), bf(), bf(), bf(), bf(), bf(), shape(width, width)),
        [SMEM] + [VMEM] * 10,
        (places, *gain, bh, bl),
        "powers",
        12,
    )
    moved, g4 = lax.optimization_barrier((moved, g4))
    mean = reach + apply(moved, 8, v8, v8_other)
    mean, g4 = lax.optimization_barrier((mean, g4))
    moved = shifted(mean, 8)
    p1, p2 = call(middle_kernel, (shape(width, width),) * 2, [VMEM], (g4,), "middle", 12)
    p4, p8, p16 = call(far_kernel, (shape(width, width),) * 3, [VMEM], (p2,), "far", 12)
    moved, p4 = lax.optimization_barrier((moved, p4))
    mean = reach + apply(moved, 8, v8, v8_other)
    mean = jnp.where(block == 0, initial_mean, mean)

    far = (p1, p2, p4, p8, p16)

    final = block == count - 1
    filtered, gap, part, back, virtual = call(
        forward_kernel,
        (
            shape(steps, trials, width),
            shape(4, steps // 4, trials, width),
            shape(4, trials, width),
            shape(trials, width),
            shape(trials, width),
        ),
        [SMEM, SMEM] + [VMEM] * 12,
        (mask, final.reshape(1).astype(jnp.int32), mean, drive, inputs, pair, bh, bl, gh, gl, g4h, g4l, kh, kl),
        "forward",
        10,
    )

    scan = lax.all_to_all(back, "tm", 0, 0, tiled=True)
    for k in range(5):
        ahead = jnp.concatenate([scan[2**k :], jnp.zeros((2**k, width), F32)], 0)
        scan = scan + ahead + high_dot(ahead, far[k])
    ahead = jnp.concatenate([scan[1:], jnp.zeros((1, width), F32)], 0)
    back_in = lax.all_to_all(ahead, "tm", 0, 0, tiled=True)
    smoothed = call(
        backward_kernel,
        shape(4, steps // 4, trials, width),
        [VMEM] * 7,
        (jnp.where(final, virtual, back_in), gap, part, gh, gl, g4h, g4l),
        "backward",
        3,
    )
    return filtered, smoothed.reshape(steps, trials, width)


def solution(mesh):
    placed = (
        P("tm", "state", None),
        P("tm"),
        P(None, "state"),
        P(None, "state"),
        P(None, "state"),
        P(),
        P("state", None),
    )
    return jax.shard_map(
        local,
        mesh=mesh,
        in_specs=placed,
        out_specs=(P("tm", "state", None), P("tm", "state", None)),
        check_vma=False,
    )
```

```python
import functools

import jax
import jax.numpy as jnp
from jax import lax
from jax.experimental import pallas as pl
from jax.experimental.pallas import tpu as pltpu
from jax.sharding import PartitionSpec as P

F32 = jnp.float32
BF16 = jnp.bfloat16
VMEM = pl.BlockSpec(memory_space=pltpu.VMEM)
SMEM = pl.BlockSpec(memory_space=pltpu.SMEM)
LIMIT = 16 * 1024 * 1024


def split(a):
    high = a.astype(BF16)
    return high, (a - high.astype(F32)).astype(BF16)


def dot(left, right):
    return jnp.dot(left, right, preferred_element_type=F32)


def dot3(a, high, low):
    rows = a.shape[0]
    a_high, a_low = split(a)
    both = dot(jnp.concatenate([a_high, a_low], 0), high)
    return both[:rows] + both[rows:] + dot(a_high, low)


def call(kernel, outs, specs, args, name, micros, scratch=(), out_specs=None):
    return pl.pallas_call(
        kernel,
        out_shape=outs,
        in_specs=specs,
        out_specs=jax.tree.map(lambda _: VMEM, outs) if out_specs is None else out_specs,
        scratch_shapes=list(scratch),
        compiler_params=pltpu.CompilerParams(vmem_limit_bytes=LIMIT),
        cost_estimate=pl.CostEstimate(flops=int(micros * 1.15e9), bytes_accessed=1 << 20, transcendentals=0),
        name=name,
    )(*args)


def shape(*dims, dtype=F32):
    return jax.ShapeDtypeStruct(dims, dtype)


def drive_kernel(mask_ref, frames_ref, gain_ref, out_ref, flags_ref):
    high, low = split(gain_ref[...])
    frames = frames_ref[...]
    turned = (((1,), (1,)), ((), ()))
    drive = lax.dot_general(frames, high, turned, preferred_element_type=F32)
    drive = drive + lax.dot_general(frames, low, turned, preferred_element_type=F32)
    steps, trials, _ = out_ref.shape
    for t in range(steps):
        out_ref[t] = drive[t * trials : (t + 1) * trials] * mask_ref[t].astype(F32)
        flags_ref[t] = mask_ref[t]


PIECES = ((0, 0), (1, 0), (2, 0), (3, 0))


def gathered(place_ref, pieces, write):
    width = pieces[0].shape[-1]
    size = pieces[0].shape[-2]
    chips = width // (2 * size)
    place = place_ref[0]
    for i, piece in enumerate(pieces):
        away, first = PIECES[i % len(PIECES)]
        panel = piece.shape[-2]
        core = lax.rem(place + (0 if i < len(PIECES) else 1), 2)
        source = 2 * lax.rem(lax.div(place, 2) + chips - away, chips) + core
        row = pl.multiple_of(source * size + first, panel)
        across = lax.broadcasted_iota(jnp.int32, (panel, width), 1)
        down = lax.broadcasted_iota(jnp.int32, (panel, width), 0) + row
        write(pl.ds(row, panel), piece, jnp.where(across == down, 1.0, 0.0).astype(F32))


def gain_kernel(place_ref, own_ref, out_ref):
    panel, width = own_ref.shape
    across = lax.broadcasted_iota(jnp.int32, (panel, width), 1)
    down = lax.broadcasted_iota(jnp.int32, (panel, width), 0) + place_ref[0] * panel
    out_ref[...] = own_ref[...] - jnp.where(across == down, 1.0, 0.0).astype(F32)


def compose(eh, el, lh, ll):
    product = dot(eh, lh) + dot(el, lh) + dot(eh, ll)
    whole = eh.astype(F32) + el.astype(F32) + lh.astype(F32) + ll.astype(F32)
    return split(product + whole)


def chosen_step(rows, flags, high_ref, low_ref):
    parts = [dot3(rows, high_ref[m], low_ref[m]) for m in range(2)]
    size = rows.shape[0] // len(flags)
    return [
        jnp.where(flag > 0, parts[1][i * size : (i + 1) * size], parts[0][i * size : (i + 1) * size])
        for i, flag in enumerate(flags)
    ]


def local_kernel(place_ref, mask_ref, *refs):
    pieces, (drive_ref, start_ref, last_ref, input_ref, high_ref, low_ref, pair_ref) = refs[:8], refs[8:]
    pairs, trials, width = input_ref.shape

    def write(rows, piece, eye):
        for m in range(2):
            high, low = split(piece[m] - eye)
            high_ref[m, rows, :] = high
            low_ref[m, rows, :] = low

    gathered(place_ref, pieces, write)

    for i in range(4):
        first, second = i % 2, i // 2
        pair_ref[i, 0], pair_ref[i, 1] = compose(high_ref[first], low_ref[first], high_ref[second], low_ref[second])
    for start in range(0, pairs, 8):
        some = range(start, start + 8)
        rows = jnp.concatenate([drive_ref[2 * i] for i in some], 0)
        moved = chosen_step(rows, [mask_ref[2 * i + 1] for i in some], high_ref, low_ref)
        for i, part in zip(some, moved):
            input_ref[i] = drive_ref[2 * i] + part + drive_ref[2 * i + 1]

    def step(i, mean):
        p = mask_ref[2 * i] + 2 * mask_ref[2 * i + 1]
        return mean + dot3(mean, pair_ref[p, 0], pair_ref[p, 1]) + input_ref[i]

    last_ref[...] = lax.fori_loop(0, pairs, step, start_ref[...], unroll=True)


def window_kernel(begin, count, core_ref, pattern_ref, pair_ref, *refs):
    out_ref = refs[-1]
    width, half = out_ref.shape
    if begin == 0:
        across = lax.broadcasted_iota(jnp.int32, (width, half), 1) + core_ref[0] * half
        down = lax.broadcasted_iota(jnp.int32, (width, half), 0)
        out_ref[...] = jnp.where(across == down, 1.0, 0.0).astype(F32)
    else:
        out_ref[...] = refs[0][...]
    end = pattern_ref.shape[0] - 2 - 2 * begin

    def step(i, _):
        p = pattern_ref[end - 2 * i] + 2 * pattern_ref[end - 2 * i + 1]

        @pl.when(p < 4)
        def _():
            high, low = split(out_ref[...])
            out_ref[...] += dot(pair_ref[p, 0], high) + dot(pair_ref[p, 1], high) + dot(pair_ref[p, 0], low)

        return 0

    lax.fori_loop(0, count, step, 0, unroll=2)


def join_kernel(core_ref, valid_ref, far_ref, far_other_ref, near_ref, near_other_ref, out_ref, out_other_ref):
    half = near_ref.shape[1]
    total, total_other = jnp.zeros(out_ref.shape, F32), jnp.zeros(out_ref.shape, F32)
    for side, part_ref in ((core_ref[0], far_ref), (1 - core_ref[0], far_other_ref)):
        rows = pl.ds(pl.multiple_of(side * half, half), half)
        part = part_ref[...]
        part_high, part_low = split(jnp.where(valid_ref[0] > 0, part, jnp.zeros_like(part)))

        def times(ref):
            high, low = split(ref[rows, :])
            return dot(part_high, high) + dot(part_low, high) + dot(part_high, low)

        total, total_other = total + times(near_ref), total_other + times(near_other_ref)
    out_ref[...], out_other_ref[...] = total, total_other


def square(ref):
    high, low = split(ref[...])
    ref[...] = 2.0 * ref[...] + dot(high, high) + dot(low, high) + dot(high, low)


def powers_kernel(place_ref, *refs):
    pieces = refs[:8]
    fh_ref, fl_ref, gh_ref, gl_ref, g4h_ref, g4l_ref, kh_ref, kl_ref, now_ref = refs[8:]

    def write(rows, piece, _):
        now_ref[rows, :] = piece[...]

    gathered(place_ref, pieces, write)
    high, low = split(now_ref[...])
    gh_ref[...], gl_ref[...] = high, low
    product = dot(fh_ref[0], high) + dot(fl_ref[0], high) + dot(fh_ref[0], low)
    both = fh_ref[0].astype(F32) + fl_ref[0].astype(F32) + now_ref[...]
    kh_ref[...], kl_ref[...] = split(product + both)
    square(now_ref)
    square(now_ref)
    g4h_ref[...], g4l_ref[...] = split(now_ref[...])


def middle_kernel(now_ref, p1_ref, p2_ref):
    p1_ref[...] = now_ref[...]
    square(p1_ref)
    square(p1_ref)
    p2_ref[...] = p1_ref[...]
    square(p2_ref)


def far_kernel(p2_ref, p4_ref, p8_ref, p16_ref):
    p4_ref[...] = p2_ref[...]
    square(p4_ref)
    p8_ref[...] = p4_ref[...]
    square(p8_ref)
    p16_ref[...] = p8_ref[...]
    square(p16_ref)


def forward_kernel(mask_ref, final_ref, start_ref, drive_ref, input_ref, pair_ref, bh_ref, bl_ref, gh_ref, gl_ref,
                   g4h_ref, g4l_ref, kh_ref, kl_ref, filtered_ref, gap_ref, part_ref, back_ref, virtual_ref):
    steps, trials, width = drive_ref.shape
    groups, inner = gap_ref.shape[:2]

    def step(i, mean):
        p = mask_ref[2 * i] + 2 * mask_ref[2 * i + 1]
        mean = mean + dot3(mean, pair_ref[p, 0], pair_ref[p, 1]) + input_ref[i]
        filtered_ref[2 * i + 1] = mean
        return mean

    last = lax.fori_loop(0, steps // 2, step, start_ref[...], unroll=True)
    for start in range(0, steps, 16):
        some = range(start, start + 16, 2)
        rows = [start_ref[...] if t == 0 else filtered_ref[t - 1] for t in some]
        moved = chosen_step(jnp.concatenate(rows, 0), [mask_ref[t] for t in some], bh_ref, bl_ref)
        for t, row, part in zip(some, rows, moved):
            filtered_ref[t] = row + part + drive_ref[t]
    virtual = last + dot3(last, bh_ref[0], bl_ref[0])
    virtual_ref[...] = virtual
    flat = filtered_ref[...].reshape(steps * trials, width)
    gap_ref[...] = -dot3(flat, kh_ref[...], kl_ref[...]).reshape(groups, inner, trials, width)
    value = gap_ref[:, inner - 1].reshape(groups * trials, width)
    for j in range(inner - 2, -1, -1):
        value = value + dot3(value, gh_ref[...], gl_ref[...]) + gap_ref[:, j].reshape(groups * trials, width)
    part = value.reshape(groups, trials, width)
    part_ref[...] = part
    carry = jnp.where(final_ref[0] > 0, virtual, jnp.zeros_like(virtual))
    for g in range(groups - 1, -1, -1):
        carry = carry + dot3(carry, g4h_ref[...], g4l_ref[...]) + part[g]
    back_ref[...] = carry


def backward_kernel(start_ref, gap_ref, part_ref, gh_ref, gl_ref, g4h_ref, g4l_ref, out_ref):
    groups, inner, trials, width = gap_ref.shape
    carry = start_ref[...]
    starts = [carry]
    for g in range(groups - 1, 0, -1):
        carry = carry + dot3(carry, g4h_ref[...], g4l_ref[...]) + part_ref[g]
        starts.insert(0, carry)
    value = jnp.concatenate(starts, 0)
    for j in range(inner - 1, -1, -1):
        value = value + dot3(value, gh_ref[...], gl_ref[...]) + gap_ref[:, j].reshape(groups * trials, width)
        out_ref[:, j] = value.reshape(groups, trials, width)


def high_dot(left, right):
    return jnp.dot(left, right, precision=lax.Precision.HIGH, preferred_element_type=F32)


def local(observations, mask, transition, updated_transition, smoother_gain, obs_gain, initial_mean):
    steps, trials, channels = observations.shape
    width, panel = transition.shape
    count = lax.axis_size("tm")
    chips = lax.axis_size("state") // 2
    block = lax.axis_index("tm")
    place = lax.axis_index("state")
    chip, core = place // 2, place % 2

    def along_x(a, k):
        return lax.ppermute(
            a, "state", [(2 * i + c, 2 * ((i + k) % chips) + c) for i in range(chips) for c in range(2)]
        )

    def swap(a):
        return lax.ppermute(a, "state", [(2 * i + c, 2 * i + 1 - c) for i in range(chips) for c in range(2)])

    def shifted(a, k):
        return lax.ppermute(a, "tm", [(i, (i + k) % count) for i in range(count)])

    def along(own):
        return [own] + [along_x(own, k) for k in (1, 2, 3)]

    own = jnp.stack([transition.T, updated_transition.T])
    mine = along(own)
    own, mine[3] = lax.optimization_barrier((own, mine[3]))
    theirs = [swap(a) for a in (own, *mine[1:])]
    places = place.reshape(1).astype(jnp.int32)

    drive, flags = call(
        drive_kernel,
        (shape(steps, trials, width), shape(steps, dtype=jnp.int32)),
        [SMEM, VMEM, VMEM],
        (mask, observations.reshape(steps * trials, channels), obs_gain),
        "drive",
        2,
        out_specs=(VMEM, SMEM),
    )
    recent = jnp.concatenate([jnp.where(block >= k, shifted(flags, k), 2) for k in (2, 1)])
    pattern = jnp.concatenate([jnp.where(block >= 2, shifted(recent, 2), 2), recent])

    start = jnp.where(block == 0, initial_mean, jnp.zeros_like(initial_mean))
    bf = functools.partial(shape, width, width, dtype=BF16)
    two = shape(2, width, width, dtype=BF16)
    last, inputs, bh, bl, pair = call(
        local_kernel,
        (shape(trials, width), shape(steps // 2, trials, width), two, two, shape(4, 2, width, width, dtype=BF16)),
        [SMEM, SMEM] + [VMEM] * 10,
        (places, mask, *mine, *theirs, drive, start),
        "local",
        9,
    )

    half = width // 2
    cores = core.reshape(1).astype(jnp.int32)

    def window(begin, count, pattern, *first):
        return call(
            functools.partial(window_kernel, begin, count),
            shape(width, half),
            [SMEM, SMEM, VMEM] + [VMEM] * len(first),
            (cores, pattern, pair, *first),
            f"window{begin + count}",
            0.6 * count,
        )

    def apply(mean, k, mine, theirs):
        mean = jnp.where(block >= k, mean, 0.0)
        here, there = high_dot(mean, mine), high_dot(mean, theirs)
        return jnp.where(
            core == 0, jnp.concatenate([here, there], 1), jnp.concatenate([there, here], 1)
        )

    one, two_back = shifted(last, 1), shifted(last, 2)
    v1 = window(0, 8, recent)
    v1_other = swap(v1)
    v2 = window(8, 8, recent, v1)
    v1, v1_other, v2 = lax.optimization_barrier((v1, v1_other, v2))
    reach = jnp.where(block >= 1, one, 0.0) + apply(two_back, 2, v1, v1_other)

    reach, v2 = lax.optimization_barrier((reach, v2))
    moved = shifted(reach, 2)
    v2_other = swap(v2)
    v4 = window(16, 8, pattern, v2)
    v2, v2_other, v4 = lax.optimization_barrier((v2, v2_other, v4))
    reach = reach + apply(moved, 2, v2, v2_other)

    reach, v4 = lax.optimization_barrier((reach, v4))
    moved = shifted(reach, 4)
    v4 = window(24, 8, pattern, v4)
    moved, v4 = lax.optimization_barrier((moved, v4))
    v4_far = shifted(v4, 4)
    v4_other = swap(v4)
    reach = reach + apply(moved, 4, v4, v4_other)
    moved = shifted(reach, 8)
    gain_own, reach = lax.optimization_barrier((smoother_gain.T, reach))
    gain_own = call(gain_kernel, shape(panel, width), [SMEM, VMEM], (places, gain_own), "gain", 8)
    gain_mine = along(gain_own)
    v4_far, *gain_mine = lax.optimization_barrier((v4_far, *gain_mine))
    v4_far_other = swap(v4_far)
    moved, *gain_mine = lax.optimization_barrier((moved, *gain_mine))
    gain_theirs = [swap(a) for a in gain_mine]
    v8, v8_other = call(
        join_kernel,
        (shape(width, half),) * 2,
        [SMEM, SMEM] + [VMEM] * 4,
        (cores, (block >= 4).reshape(1).astype(jnp.int32), v4_far, v4_far_other, v4, v4_other),
        "join",
        1.5,
    )
    mean = reach + apply(moved, 8, v8, v8_other)
    gain_mine[0], mean = lax.optimization_barrier((gain_mine[0], mean))
    gain = [*gain_mine, *gain_theirs]
    moved = shifted(mean, 8)
    gh, gl, g4h, g4l, kh, kl, g4 = call(
        powers_kernel,
        (bf(), bf(), bf(), bf(), bf(), bf(), shape(width, width)),
        [SMEM] + [VMEM] * 10,
        (places, *gain, bh, bl),
        "powers",
        12,
    )
    moved, g4 = lax.optimization_barrier((moved, g4))
    mean = reach + apply(moved, 8, v8, v8_other)
    mean, g4 = lax.optimization_barrier((mean, g4))
    moved = shifted(mean, 8)
    p1, p2 = call(middle_kernel, (shape(width, width),) * 2, [VMEM], (g4,), "middle", 12)
    p4, p8, p16 = call(far_kernel, (shape(width, width),) * 3, [VMEM], (p2,), "far", 12)
    moved, p4 = lax.optimization_barrier((moved, p4))
    mean = reach + apply(moved, 8, v8, v8_other)
    mean = jnp.where(block == 0, initial_mean, mean)

    far = (p1, p2, p4, p8, p16)

    final = block == count - 1
    filtered, gap, part, back, virtual = call(
        forward_kernel,
        (
            shape(steps, trials, width),
            shape(4, steps // 4, trials, width),
            shape(4, trials, width),
            shape(trials, width),
            shape(trials, width),
        ),
        [SMEM, SMEM] + [VMEM] * 12,
        (mask, final.reshape(1).astype(jnp.int32), mean, drive, inputs, pair, bh, bl, gh, gl, g4h, g4l, kh, kl),
        "forward",
        10,
    )

    scan = lax.all_to_all(back, "tm", 0, 0, tiled=True)
    for k in range(5):
        ahead = jnp.concatenate([scan[2**k :], jnp.zeros((2**k, width), F32)], 0)
        scan = scan + ahead + high_dot(ahead, far[k])
    ahead = jnp.concatenate([scan[1:], jnp.zeros((1, width), F32)], 0)
    back_in = lax.all_to_all(ahead, "tm", 0, 0, tiled=True)
    smoothed = call(
        backward_kernel,
        shape(4, steps // 4, trials, width),
        [VMEM] * 7,
        (jnp.where(final, virtual, back_in), gap, part, gh, gl, g4h, g4l),
        "backward",
        3,
    )
    return filtered, smoothed.reshape(steps, trials, width)


def solution(mesh):
    placed = (
        P("tm", "state", None),
        P("tm"),
        P(None, "state"),
        P(None, "state"),
        P(None, "state"),
        P(),
        P("state", None),
    )
    return jax.shard_map(
        local,
        mesh=mesh,
        in_specs=placed,
        out_specs=(P("tm", "state", None), P("tm", "state", None)),
        check_vma=False,
    )
```
